256 devices in a mesh: dom: 64 (over z, x, core), blk: 4 (over y).
Axes of the slice: x: 4, y: 4, z: 8, core: 2. Of those that a mesh axis runs over, the one named last changes fastest.
Arguments:
- residual: float32 [4096, 135], P(('dom', 'blk')), may hold values from -112.5 to 112.5
- recycle_basis: float32 [8, 4096, 135], P(None, ('dom', 'blk')), may hold values from -5 to 5
- recycle_images: float32 [8, 4096, 135], P(None, ('dom', 'blk')), may hold values from -5 to 5
- jacobian: float32 [4096, 7, 135, 135], P(('dom', 'blk')), may hold values from -1.5 to 5.5
- neighbours: int32 [4096, 6], P(('dom', 'blk')), may hold values from -1 to 4095, as said below
- line_members: int32 [512, 8], replicated, may hold values from 0 to 4095, as said below
- line_pivots: float32 [512, 8, 135, 135], P(('dom', 'blk')), may hold values from -0.2 to 0.4
- line_lower: float32 [512, 7, 135, 135], P(('dom', 'blk')), may hold values from -0.375 to 0.375
- line_upper: float32 [512, 7, 135, 135], P(('dom', 'blk')), may hold values from -0.125 to 0.125
Outputs:
- correction: float32 [4096, 135], P(('dom', 'blk'))
- basis: float32 [9, 4096, 135], P(None, ('dom', 'blk'))
- hessenberg: float32 [9, 8], replicated
- residual_norm: float32 [], replicated
The draws below stay inside these ranges and needn't reach their ends.
Inputs may be any that keep to these rules, and one draw needn't show every extreme that they name: `line_members`: each element lies in exactly one line. The lines of partition p (the 64 elements p * 64 to (p+1) * 64 - 1 on dom index p) are lines p * 8 onwards; they take exactly 8 elements from partition p-1, exactly 8 from partition p+1 (the first and last partition counting as beside each other) and all others from partition p. `neighbours`: every face neighbour lies in the element's own partition or in one of the two partitions beside it along dom, the first and last partition counting as beside each other.
All inputs are finite; a program needn't handle non-finite values.
Results may differ from the reference program's by a relative error of at most 0.0055.
Values sent between devices are 32-bit elements; how exact they have to be, the bound alone decides.
No kernel may reach another device: no remote copies, remote signals or barrier semaphores. Data moves between devices by JAX's collectives and lax.ppermute only.
A program may use at most 128 MiB of HBM per device.

```python
import math
import jax
import jax.numpy as jnp
from jax import lax

ELEM_DOFS = 135
LINE_LEN = 8
ARNOLDI_STEPS = 8
RECYCLED = 8
ELEM_PART = 64
ELEMENTS = 4096
LINE_COUNT = 512
PEER_SENDS = 8


def shared_images(key):
    images = jax.random.normal(key, (RECYCLED, ELEMENTS, ELEM_DOFS), jnp.float32)
    return jnp.clip(images, -5.0, 5.0)


def draw_recycle_images(key, part):
    images = shared_images(key)
    return images


def draw_residual(key, part):
    images = shared_images(key)
    key = jax.random.fold_in(key, 37)
    first, second, third = jax.random.split(key, 3)
    weights = jnp.clip(jax.random.normal(first, (RECYCLED,), jnp.float32), -2.5, 2.5)
    spread = jnp.exp(jax.random.uniform(second, (ELEMENTS, 1), jnp.float32, 0.0, math.log(10.0)))
    rough = jnp.clip(jax.random.normal(third, (ELEMENTS, ELEM_DOFS), jnp.float32), -4.0, 4.0)
    return jnp.sum(weights[:, None, None] * images, 0) + 0.3 * spread * rough


def draw_jacobian(key, part):
    key = jax.random.fold_in(key, 29)
    first = jax.random.fold_in(key, 0)
    shape = (ELEMENTS, 7, ELEM_DOFS, ELEM_DOFS)
    noise = jnp.clip(jax.random.normal(first, shape, jnp.float32), -4.0, 4.0)
    faces = jnp.ones((ELEMENTS, 1, 1, 1), jnp.float32)
    block_scale = jnp.concatenate([jnp.ones((1,), jnp.float32), 0.4 * jnp.ones((6,), jnp.float32)])
    block_scale = block_scale[None, :, None, None] * jnp.where(jnp.arange(7)[None, :, None, None] == 0, 1.0, faces)
    diagonal = jnp.where(jnp.arange(7)[:, None, None] == 0, 4.0, 0.0) * jnp.eye(ELEM_DOFS, dtype=jnp.float32)[None]
    return diagonal[None] + block_scale * noise / ELEM_DOFS ** 0.5


def draw_line_pivots(key, part):
    key = jax.random.fold_in(key, 23)
    shape = (LINE_COUNT, LINE_LEN, ELEM_DOFS, ELEM_DOFS)
    noise = jnp.clip(jax.random.normal(key, shape, jnp.float32), -4.0, 4.0)
    return 0.25 * jnp.eye(ELEM_DOFS, dtype=jnp.float32) + 0.125 / ELEM_DOFS ** 0.5 * noise


def draw_neighbours(key, part):
    key = jax.random.fold_in(key, 11)
    first, second, third = jax.random.split(key, 3)
    dom_count = ELEMENTS // ELEM_PART
    owner = jnp.arange(ELEMENTS, dtype=jnp.int32) // ELEM_PART
    offset = jax.random.randint(first, (ELEMENTS, 6), -1, 2, dtype=jnp.int32)
    partition = (owner[:, None] + offset + dom_count) % dom_count
    within = jax.random.randint(second, (ELEMENTS, 6), 0, ELEM_PART, dtype=jnp.int32)
    ids = partition * ELEM_PART + within
    walls = jax.random.randint(third, (ELEMENTS, 6), 0, 8, dtype=jnp.int32) == 0
    ids = jnp.where(walls, -1, ids)
    ids = ids.at[0, 0].set(ELEMENTS - 1).at[0, 1].set(-1)
    return ids.astype(jnp.int32)


def draw_line_members(key, part):
    key = jax.random.fold_in(key, 17)
    first, second = jax.random.split(key)
    dom_count = ELEMENTS // ELEM_PART
    shuffled = jax.vmap(lambda single: jax.random.permutation(single, ELEM_PART))(jax.random.split(first, dom_count))
    shuffled = shuffled.astype(jnp.int32) + (jnp.arange(dom_count, dtype=jnp.int32) * ELEM_PART)[:, None]
    to_left = shuffled[:, :PEER_SENDS]
    to_right = shuffled[:, PEER_SENDS:2 * PEER_SENDS]
    keep = shuffled[:, 2 * PEER_SENDS:]
    pool = jnp.concatenate([keep, jnp.roll(to_right, 1, 0), jnp.roll(to_left, -1, 0)], 1)
    order = jax.vmap(lambda single: jax.random.permutation(single, ELEM_PART))(jax.random.split(second, dom_count))
    lines = jnp.take_along_axis(pool, order.astype(jnp.int32), 1)
    return lines.reshape(LINE_COUNT, LINE_LEN).astype(jnp.int32)


def level_of(key, shape, cuts, least, top_value):
    level = 1.0
    for axis_at, parts in cuts:
        draws = jax.random.uniform(jax.random.fold_in(jax.random.fold_in(key, 6), axis_at), (parts,), jnp.float32, least / len(cuts), top_value / len(cuts))
        level = level * jnp.repeat(jnp.exp(draws), shape[axis_at] // parts).reshape((-1,) + (1,) * (len(shape) - 1 - axis_at))
    return level


def gaussian(rng, shape, deviation, limit, pieces=(), held_as=jnp.bfloat16):
    values = jax.random.normal(rng, shape, jnp.float32) * deviation
    if len(pieces) > 0:
        values = level_of(rng, shape, pieces, -0.22, 0.18) * values
    return jnp.clip(values, min=-limit, max=limit).astype(held_as)


def setup_inputs(seed: int = 0) -> dict:
    splits = jax.random.split(jax.random.key(seed), 10)
    residual = draw_residual(jax.random.fold_in(splits[9], 71), 0)
    recycle_basis = gaussian(splits[1], (RECYCLED, ELEMENTS, ELEM_DOFS), 1.0, 5.0, ((1, 256),), jnp.float32)
    recycle_images = draw_recycle_images(jax.random.fold_in(splits[9], 71), 0)
    jacobian = draw_jacobian(jax.random.fold_in(splits[9], 71), 0)
    neighbours = draw_neighbours(jax.random.fold_in(splits[9], 71), 0)
    line_members = draw_line_members(jax.random.fold_in(splits[9], 71), 0)
    line_pivots = draw_line_pivots(jax.random.fold_in(splits[9], 71), 0)
    line_lower = gaussian(splits[7], (LINE_COUNT, LINE_LEN - 1, ELEM_DOFS, ELEM_DOFS), (2 * ELEM_DOFS) ** -0.5, 0.375, ((0, 256),), jnp.float32)
    line_upper = gaussian(splits[8], (LINE_COUNT, LINE_LEN - 1, ELEM_DOFS, ELEM_DOFS), (16 * ELEM_DOFS) ** -0.5, 0.125, ((0, 256),), jnp.float32)
    return {"residual": residual, "recycle_basis": recycle_basis, "recycle_images": recycle_images, "jacobian": jacobian, "neighbours": neighbours, "line_members": line_members, "line_pivots": line_pivots, "line_lower": line_lower, "line_upper": line_upper}


highest = lax.Precision.HIGHEST
epsilon = 1e-06

def line_solve(line_rhs, line_pivots, line_lower, line_upper):
    length = line_rhs.shape[1]
    forward = [jnp.einsum('lij,lj->li', line_pivots[:, 0], line_rhs[:, 0], precision=highest)]
    for level in range(1, length):
        carried = line_rhs[:, level] - jnp.einsum('lij,lj->li', line_lower[:, level - 1], forward[-1], precision=highest)
        forward.append(jnp.einsum('lij,lj->li', line_pivots[:, level], carried, precision=highest))
    result = [forward[-1]]
    for level in range(length - 2, -1, -1):
        result.insert(0, forward[level] - jnp.einsum('lij,lj->li', line_upper[:, level], result[0], precision=highest))
    return jnp.stack(result, 1)

def precondition(vector, line_members, line_pivots, line_lower, line_upper):
    flat_members = line_members.reshape(-1)
    line_rhs = vector[flat_members].reshape(line_members.shape[0], line_members.shape[1], vector.shape[1])
    solved = line_solve(line_rhs, line_pivots, line_lower, line_upper)
    restore = jnp.argsort(flat_members)
    return solved.reshape(-1, vector.shape[1])[restore]

def apply_operator(field, jacobian, neighbours):
    present = neighbours >= 0
    clamped = jnp.where(present, neighbours, 0)
    beside = field[clamped] * present[..., None].astype(field.dtype)
    stacked = jnp.concatenate([field[:, None], beside], 1)
    return jnp.einsum('efij,efj->ei', jacobian, stacked, precision=highest)

def reference(residual, recycle_basis, recycle_images, jacobian, neighbours, line_members, line_pivots, line_lower, line_upper):
    entries = residual.shape[0] * residual.shape[1]
    coefficients = jnp.einsum('kej,ej->k', recycle_images, residual, precision=highest) / entries
    correction = jnp.einsum('k,kej->ej', coefficients, recycle_basis, precision=highest)
    start = residual - jnp.einsum('k,kej->ej', coefficients, recycle_images, precision=highest)
    residual_norm = jnp.sqrt(jnp.sum(start * start) / entries + epsilon)
    vectors = [start / residual_norm]
    hessenberg = jnp.zeros((ARNOLDI_STEPS + 1, ARNOLDI_STEPS), jnp.float32)
    for column in range(ARNOLDI_STEPS):
        applied = apply_operator(precondition(vectors[-1], line_members, line_pivots, line_lower, line_upper), jacobian, neighbours)
        stacked = jnp.stack(vectors)
        projection = jnp.einsum('bej,ej->b', stacked, applied, precision=highest) / entries
        reduced = applied - jnp.einsum('b,bej->ej', projection, stacked, precision=highest)
        subdiag = jnp.sqrt(jnp.sum(reduced * reduced) / entries + epsilon)
        hessenberg = hessenberg.at[:column + 1, column].set(projection)
        hessenberg = hessenberg.at[column + 1, column].set(subdiag)
        vectors.append(reduced / subdiag)
    return (correction, jnp.stack(vectors), hessenberg, residual_norm)
```

```python
import functools

import jax
import jax.numpy as jnp
from jax import lax
from jax.experimental import pallas as pl
from jax.experimental.pallas import tpu as pltpu
from jax.sharding import PartitionSpec as P

STEPS = 8
EPS = 1e-06
LANES = 128
ROWS = 136
INTERPRET = False
f32 = jnp.float32
bf16 = jnp.bfloat16
MIB = 1024 * 1024


def vmem_out(shape):
    if INTERPRET:
        return jax.ShapeDtypeStruct(shape, f32)
    return pltpu.VMEM(shape, f32)


def in_vmem(array):
    return array if INTERPRET else pltpu.with_memory_space_constraint(array, pltpu.VMEM)


def call(body, out_shape, *args, scratch=(), limit=24, specs=None):
    spec = pl.BlockSpec(memory_space=pltpu.VMEM)
    outs = out_shape if isinstance(out_shape, (list, tuple)) else None
    return pl.pallas_call(
        body,
        out_shape=out_shape,
        in_specs=specs if specs is not None else [spec] * len(args),
        out_specs=[spec] * len(outs) if outs is not None else spec,
        scratch_shapes=list(scratch),
        compiler_params=pltpu.CompilerParams(vmem_limit_bytes=limit * MIB),
        interpret=INTERPRET,
    )(*args)


def pick(hits, pool):
    hits = hits.astype(bf16)
    high = pool.astype(bf16)
    rest = pool - high.astype(f32)
    mid = rest.astype(bf16)
    low = (rest - mid.astype(f32)).astype(bf16)
    dot = functools.partial(jnp.dot, preferred_element_type=f32)
    return dot(hits, high) + (dot(hits, mid) + dot(hits, low))


def halves(array):
    high = array.astype(bf16)
    return high, (array - high.astype(f32)).astype(bf16)


def product(left, right, dims):
    lh, ll = halves(left)
    rh, rl = halves(right)
    dot = lambda a, b: lax.dot_general(a, b, (dims, ((), ())), preferred_element_type=f32)
    return dot(lh, rh) + (dot(lh, rl) + dot(ll, rh))


def pack_body(jac_hbm, main_ref, rest_ref):
    faces, rows, elems, cols = jac_hbm.shape
    chunk = 27
    extra = cols - LANES

    def step(block, at=None):
        at = (pl.program_id(0) if at is None else at) * chunk
        lane = lax.broadcasted_iota(jnp.int32, (elems, LANES), 1)

        def row(i, _):
            packed = jnp.zeros((elems, LANES), f32)
            for f in range(faces):
                main_ref[f, at + i] = block[f, i, :, 0:LANES]
                tail = jnp.concatenate(
                    [block[f, i, :, LANES:cols], jnp.zeros((elems, LANES - extra), f32)], 1
                )
                if f:
                    tail = pltpu.roll(tail, f * extra, 1)
                packed = packed + tail
            rest_ref[at + i] = packed
            return 0

        lax.fori_loop(0, chunk, row, 0)

    if INTERPRET:
        for c in range(rows // chunk):
            step(jac_hbm[:, c * chunk : (c + 1) * chunk], c)
        return
    pltpu.emit_pipeline(
        step,
        grid=(rows // chunk,),
        in_specs=[pl.BlockSpec((faces, chunk, elems, cols), lambda c: (0, c, 0, 0))],
    )(jac_hbm)


def invert_body(pivot_ref, lower_ref, upper_ref, main_ref, rest_ref, part_ref, wide_ref, side_ref):
    lines, levels, height, _ = main_ref.shape
    cols = part_ref.shape[2]
    extra = cols - LANES
    rows_by_rows = ((1,), (1,))
    rows_by_cols = ((1,), (0,))
    pivot_rows, pair_rows = levels * cols, lines * cols

    def line(l, _):
        wide_ref[0:pivot_rows, :] = pivot_ref[l, :, 0:LANES]
        side_ref[0:pivot_rows, 0:extra] = pivot_ref[l, :, LANES:cols]

        def strided(first, count):
            at = pl.ds(first, cols, stride=count)
            return jnp.concatenate([wide_ref[at, :], side_ref[at, :][:, 0:extra]], 1)

        def pivot_of(k):
            return strided(k, levels)

        def paired(ref, k):
            wide_ref[pivot_rows:, :] = ref[k, :, 0:LANES]
            side_ref[pivot_rows:, 0:extra] = ref[k, :, LANES:cols]
            return strided(pivot_rows + l, lines)

        part_ref[...] = jnp.zeros(part_ref.shape, f32)
        part_ref[0, 0:cols, :] = pivot_of(0).T

        def forward(k, _):
            pivot = pivot_of(k)
            mixed = product(pivot, paired(lower_ref, k - 1), rows_by_cols)
            part_ref[k] = -product(part_ref[k - 1], mixed, rows_by_rows)
            part_ref[k, pl.ds(pl.multiple_of(k * ROWS, 8), cols), :] = pivot.T
            return 0

        lax.fori_loop(1, levels, forward, 0)

        def backward(i, _):
            k = levels - 2 - i
            part_ref[k] = part_ref[k] - product(
                part_ref[k + 1], paired(upper_ref, k), rows_by_rows
            )
            return 0

        lax.fori_loop(0, levels - 1, backward, 0)

        def emit(t, _):
            at = pl.ds(pl.multiple_of(t * ROWS, 8), ROWS)
            packed = jnp.zeros((ROWS, LANES), f32)
            for k in range(levels):
                main_ref[l, k, at, :] = part_ref[k, at, 0:LANES]
                tail = jnp.concatenate(
                    [part_ref[k, at, LANES:cols], jnp.zeros((ROWS, LANES - extra), f32)], 1
                )
                packed = packed + (pltpu.roll(tail, k * extra, 1) if k else tail)
            rest_ref[l, at, :] = packed
            return 0

        lax.fori_loop(0, levels, emit, 0)
        return 0

    lax.fori_loop(0, lines, line, 0)


def solve_body(*refs):
    *blocks, hits_ref, main_ref, rest_ref, out_ref, pool_ref = refs
    lines, levels, height, _ = main_ref.shape
    count, cols = blocks[0].shape
    extra = cols - LANES
    for n, block in enumerate(blocks):
        pool_ref[n * count : (n + 1) * count, :] = block[...]
    rhs = pick(hits_ref[...], pool_ref[...])
    rhs = jnp.concatenate([rhs, jnp.zeros((count, 2 * LANES - cols), f32)], 1)
    rhs = rhs.T[0:ROWS]
    for l in range(lines):
        sums = [jnp.zeros((8, LANES), f32)] * (levels + 1)
        for m in range(levels):
            column = jnp.broadcast_to(rhs[:, l * levels + m : l * levels + m + 1], (ROWS, LANES))
            for t in range(ROWS // 8):
                at = m * ROWS + t * 8
                value = column[t * 8 : t * 8 + 8]
                for k in range(levels):
                    sums[k] = sums[k] + main_ref[l, k, at : at + 8, :] * value
                sums[levels] = sums[levels] + rest_ref[l, at : at + 8, :] * value
        tails = jnp.sum(sums[levels], axis=0, keepdims=True)
        tails = jnp.broadcast_to(tails, (8, LANES))
        for k in range(levels):
            out_ref[l * levels + k : l * levels + k + 1, 0:LANES] = jnp.sum(
                sums[k], axis=0, keepdims=True
            )
            tail = pltpu.roll(tails, LANES - k * extra, 1) if k else tails
            out_ref[l * levels + k : l * levels + k + 1, LANES:cols] = tail[0:1, 0:extra]


def operate(blocks, hits_ref, main_ref, rest_ref, pool_ref):
    faces, rows, elems, _ = main_ref.shape
    count, cols = blocks[0].shape
    extra = cols - LANES
    for n, block in enumerate(blocks):
        pool_ref[n * count : (n + 1) * count, :] = block[...]
    field = pick(hits_ref[...], pool_ref[...])
    heads = [field[f * elems : (f + 1) * elems, 0:LANES] for f in range(faces)]
    packed = jnp.zeros((elems, LANES), f32)
    for f in range(faces):
        tail = jnp.concatenate(
            [field[f * elems : (f + 1) * elems, LANES:cols], jnp.zeros((elems, LANES - extra), f32)], 1
        )
        packed = packed + (pltpu.roll(tail, f * extra, 1) if f else tail)
    lane = lax.broadcasted_iota(jnp.int32, (elems, LANES), 1)

    def one(i):
        total = rest_ref[i] * packed
        for f in range(faces):
            total = total + main_ref[f, i] * heads[f]
        return jnp.sum(total, axis=1, keepdims=True)

    group = 16

    def some(g, image):
        for s in range(group):
            i = g * group + s
            image = jnp.where(lane == i, one(i), image)
        return image

    image = lax.fori_loop(0, LANES // group, some, jnp.zeros((elems, LANES), f32))
    tail = jnp.zeros((elems, LANES), f32)
    for c in range(extra):
        tail = jnp.where(lane == c, one(LANES + c), tail)
    return jnp.concatenate([image, tail[:, 0:extra]], 1)


def row_of(values):
    lane = lax.broadcasted_iota(jnp.int32, (1, LANES), 1)
    row = jnp.zeros((1, LANES), f32)
    for i, value in values.items():
        total = jnp.sum(jnp.sum(value, axis=0, keepdims=True), axis=1, keepdims=True)
        row = jnp.where(lane == i, total, row)
    return row


def lane_of(row, i):
    return row[:, i : i + 1]


UU, CC = 14, 15


def totals(parts_ref):
    return jnp.sum(parts_ref[...], axis=0, keepdims=True)


def project_body(images_ref, residual_ref, out_ref):
    residual = residual_ref[...]
    out_ref[...] = row_of({k: images_ref[k] * residual for k in range(images_ref.shape[0])})


def deflate_body(entries, parts_ref, residual_ref, basis_ref, images_ref, correction_ref, start_ref):
    row = totals(parts_ref) / entries
    correction = jnp.zeros(residual_ref.shape, f32)
    start = residual_ref[...]
    for k in range(basis_ref.shape[0]):
        weight = lane_of(row, k)
        correction = correction + weight * basis_ref[k]
        start = start - weight * images_ref[k]
    correction_ref[...] = correction
    start_ref[...] = start


def first_body(*refs):
    *blocks, u_ref, hits_ref, main_ref, rest_ref, c_ref, part_ref, pool_ref = refs
    c = operate(blocks, hits_ref, main_ref, rest_ref, pool_ref)
    c_ref[...] = c
    u = u_ref[...]
    part_ref[...] = row_of({0: u * c, UU: u * u, CC: c * c})


def advance(j, entries, row, u, c, shift, scale, basis, images, w):
    norm = jnp.sqrt(lane_of(row, UU) / entries + EPS / (scale * scale))
    inverse = 1.0 / norm
    below = scale * norm
    here = u * inverse
    image = c * inverse
    lane = lax.broadcasted_iota(jnp.int32, (1, LANES), 1)
    column = jnp.where(lane < j, row * inverse / entries, 0.0)
    own = lane_of(row, j) * inverse * inverse / entries
    column = jnp.where(lane == j, own, column)
    scale_next = jnp.sqrt(lane_of(row, CC) * inverse * inverse / entries + EPS)
    shrink = 1.0 / scale_next
    reduced = image - own * here
    for i in range(j):
        reduced = reduced - lane_of(column, i) * basis[i]
    u_next = reduced * shrink
    if w is None:
        return here, image, column, below, u_next, None, None, scale_next
    moved = w * inverse - (own - shift) * image
    for i in range(j):
        moved = moved - lane_of(column, i) * images[i]
    return here, image, column, below, u_next, moved * shrink, own, scale_next


def scalars(values):
    lane = lax.broadcasted_iota(jnp.int32, (1, LANES), 1)
    row = jnp.zeros((1, LANES), f32)
    for i, value in enumerate(values):
        row = jnp.where(lane == i, value, row)
    return row


def next_body(j, entries, *refs):
    n = 20
    blocks, refs = refs[:n], refs[n:]
    hits_ref, main_ref, rest_ref, sums_ref, u_ref, c_ref, known_ref = refs[:7]
    basis, images = refs[7 : 7 + j], refs[7 + j : 7 + 2 * j]
    (here_ref, image_ref, column_ref, below_ref, u_out, c_out, v_out, known_out, part_ref, pool_ref) = refs[
        7 + 2 * j :
    ]
    w = operate(blocks, hits_ref, main_ref, rest_ref, pool_ref)
    known = known_ref[...]
    basis = [b[...] for b in basis]
    images = [a[...] for a in images]
    here, image, column, below, u, c, shift, scale = advance(
        j,
        entries,
        totals(sums_ref),
        u_ref[...],
        c_ref[...],
        lane_of(known, 0),
        lane_of(known, 1),
        basis,
        images,
        w,
    )
    here_ref[...] = here
    image_ref[...] = image
    column_ref[...] = column
    below_ref[...] = jnp.broadcast_to(below, (1, LANES))
    u_out[...] = u
    c_out[...] = c
    v_out[...] = c - shift * u
    known_out[...] = scalars([shift, scale])
    products = {i: b * c for i, b in enumerate(basis + [here])}
    products.update({j + 1: u * c, UU: u * u, CC: c * c})
    part_ref[...] = row_of(products)


def last_body(j, entries, *refs):
    sums_ref, u_ref, c_ref, known_ref = refs[:4]
    basis = [b[...] for b in refs[4 : 4 + j]]
    here_ref, column_ref, below_ref, u_out, known_out, part_ref = refs[4 + j :]
    known = known_ref[...]
    here, _, column, below, u, _, _, scale = advance(
        j,
        entries,
        totals(sums_ref),
        u_ref[...],
        c_ref[...],
        lane_of(known, 0),
        lane_of(known, 1),
        basis,
        None,
        None,
    )
    here_ref[...] = here
    column_ref[...] = column
    below_ref[...] = jnp.broadcast_to(below, (1, LANES))
    u_out[...] = u
    known_out[...] = scalars([scale, scale])
    part_ref[...] = row_of({UU: u * u})


def finish_body(entries, *refs):
    sums_ref, u_ref, known_ref = refs[:3]
    basis = refs[3 : 3 + STEPS]
    columns = refs[3 + STEPS : 3 + 2 * STEPS]
    belows = refs[3 + 2 * STEPS : 3 + 3 * STEPS]
    basis_ref, hess_ref, norm_ref = refs[3 + 3 * STEPS :]
    scale = lane_of(known_ref[...], 1)
    norm = jnp.sqrt(lane_of(totals(sums_ref), UU) / entries + EPS / (scale * scale))
    for i in range(STEPS):
        basis_ref[i] = basis[i][...]
    basis_ref[STEPS] = u_ref[...] * (1.0 / norm)
    lane = lax.broadcasted_iota(jnp.int32, (1, LANES), 1)
    for j in range(STEPS):
        below = belows[j + 1][...] if j + 1 < STEPS else scale * norm
        hess_ref[j : j + 1, :] = jnp.where(lane == j + 1, below, columns[j][...])
    norm_ref[...] = belows[0][...]


def shifted(array, d_dom, d_blk):
    doms, blks = lax.axis_size("dom"), lax.axis_size("blk")
    if d_dom == 0 and d_blk == 0:
        return array
    pairs = []
    for d in range(doms):
        for b in range(blks):
            source = ((d + d_dom) % doms) * blks + (b + d_blk) % blks
            pairs.append((source, d * blks + b))
    return lax.ppermute(array, ("dom", "blk"), pairs)


def surroundings(array, reach):
    blks = lax.axis_size("blk")
    return [shifted(array, d, b) for d in range(-reach, reach + 1) for b in range(blks)]


def gathered(part):
    return lax.all_gather(part, ("dom", "blk"), axis=0, tiled=True)


def per_device(residual, recycle_basis, recycle_images, jacobian, neighbours, line_members,
               line_pivots, line_lower, line_upper):
    elems, cols = residual.shape
    doms, blks = lax.axis_size("dom"), lax.axis_size("blk")
    faces = jacobian.shape[1]
    lines, levels = line_pivots.shape[:2]
    entries = float(elems * cols * doms * blks)
    dom, blk = lax.axis_index("dom"), lax.axis_index("blk")
    devices = doms * blks

    row = jax.ShapeDtypeStruct((1, LANES), f32)
    rows = jax.ShapeDtypeStruct((elems, cols), f32)
    projected = gathered(call(project_body, row, recycle_images, residual))

    members = line_members.reshape(devices, elems)
    near = jnp.array([(d, b) for d in range(-2, 3) for b in range(blks)], jnp.int32)
    at = (dom + near[:, 0] + doms) % doms * blks + (blk + near[:, 1]) % blks
    line_ids = members[at].reshape(-1)
    near_own = at[blks : 4 * blks]
    elem_ids = (near_own[:, None] * elems + jnp.arange(elems, dtype=jnp.int32)).reshape(-1)
    me = dom * blks + blk
    own_ids = me * elems + jnp.arange(elems, dtype=jnp.int32)
    wanted = jnp.concatenate([own_ids[None], neighbours.T], 0).reshape(-1)
    stencil = (wanted[:, None] == line_ids[None, :]).astype(f32)
    mine = lax.dynamic_slice_in_dim(members, me, 1, 0)[0]
    entering = (mine[:, None] == elem_ids[None, :]).astype(f32)

    spec = pl.BlockSpec(memory_space=pltpu.VMEM)
    hbm = pl.BlockSpec(memory_space=pl.ANY)
    jac = jnp.transpose(jacobian, (1, 2, 0, 3))
    jac_main, jac_rest = call(
        pack_body,
        [vmem_out((faces, cols, elems, LANES)), vmem_out((cols, elems, LANES))],
        jac,
        specs=[spec if INTERPRET else hbm],
        limit=24,
    )
    pivots = jnp.transpose(line_pivots, (0, 2, 1, 3)).reshape(lines, cols * levels, cols)
    lower = jnp.transpose(line_lower, (1, 2, 0, 3)).reshape(levels - 1, cols * lines, cols)
    upper = jnp.transpose(line_upper, (1, 2, 0, 3)).reshape(levels - 1, cols * lines, cols)
    height = levels * ROWS
    inv_main, inv_rest = call(
        invert_body,
        [vmem_out((lines, levels, height, LANES)), vmem_out((lines, height, LANES))],
        pivots,
        lower,
        upper,
        scratch=[
            pltpu.VMEM((levels, height, cols), f32),
            pltpu.VMEM(((levels + lines) * cols, LANES), f32),
            pltpu.VMEM(((levels + lines) * cols, LANES), f32),
        ],
        limit=40,
    )
    jac_main, jac_rest, inv_main, inv_rest = map(in_vmem, (jac_main, jac_rest, inv_main, inv_rest))

    correction, u = call(
        functools.partial(deflate_body, entries),
        [rows, rows],
        projected,
        residual,
        recycle_basis,
        recycle_images,
    )

    def precondition(v):
        near = surroundings(v, 1)
        z = call(
            solve_body,
            rows,
            *near,
            entering,
            inv_main,
            inv_rest,
            scratch=[pltpu.VMEM((len(near) * elems, cols), f32)],
        )
        return surroundings(z, 2)

    stencil_pool = pltpu.VMEM((5 * blks * elems, cols), f32)
    matrices = (stencil, jac_main, jac_rest)
    c, part = call(
        first_body, [rows, row], *precondition(u), u, *matrices, scratch=[stencil_pool]
    )
    v = c
    known = jnp.zeros((1, LANES), f32).at[0, 1].set(1.0)
    basis, images, columns, belows = [], [], [], []
    for j in range(STEPS - 1):
        sums = gathered(part)
        here, image, column, below, u, c, v, known, part = call(
            functools.partial(next_body, j, entries),
            [rows, rows, row, row, rows, rows, rows, row, row],
            *precondition(v),
            *matrices,
            sums,
            u,
            c,
            known,
            *basis,
            *images,
            scratch=[stencil_pool],
        )
        basis.append(here)
        images.append(image)
        columns.append(column)
        belows.append(below)
    here, column, below, u, known, part = call(
        functools.partial(last_body, STEPS - 1, entries),
        [rows, row, row, rows, row, row],
        gathered(part),
        u,
        c,
        known,
        *basis,
    )
    basis.append(here)
    columns.append(column)
    belows.append(below)
    out, hess, norm = call(
        functools.partial(finish_body, entries),
        [
            jax.ShapeDtypeStruct((STEPS + 1, elems, cols), f32),
            jax.ShapeDtypeStruct((STEPS, LANES), f32),
            row,
        ],
        gathered(part),
        u,
        known,
        *basis,
        *columns,
        *belows,
    )
    return correction, out, hess[:, : STEPS + 1].T, norm[0, 0]


def solution(mesh):
    both = ("dom", "blk")
    in_specs = (
        P(both, None),
        P(None, both, None),
        P(None, both, None),
        P(both, None, None, None),
        P(both, None),
        P(),
        P(both, None, None, None),
        P(both, None, None, None),
        P(both, None, None, None),
    )
    out_specs = (P(both, None), P(None, both, None), P(), P())
    return jax.shard_map(
        per_device, mesh=mesh, in_specs=in_specs, out_specs=out_specs, check_vma=False
    )
```

```python
import functools

import jax
import jax.numpy as jnp
from jax import lax
from jax.experimental import pallas as pl
from jax.experimental.pallas import tpu as pltpu
from jax.sharding import PartitionSpec as P

STEPS = 8
EPS = 1e-06
LANES = 128
ROWS = 136
INTERPRET = False
f32 = jnp.float32
bf16 = jnp.bfloat16
MIB = 1024 * 1024


def vmem_out(shape):
    if INTERPRET:
        return jax.ShapeDtypeStruct(shape, f32)
    return pltpu.VMEM(shape, f32)


def in_vmem(array):
    return array if INTERPRET else pltpu.with_memory_space_constraint(array, pltpu.VMEM)


def call(body, out_shape, *args, scratch=(), limit=24, specs=None):
    spec = pl.BlockSpec(memory_space=pltpu.VMEM)
    outs = out_shape if isinstance(out_shape, (list, tuple)) else None
    return pl.pallas_call(
        body,
        out_shape=out_shape,
        in_specs=specs if specs is not None else [spec] * len(args),
        out_specs=[spec] * len(outs) if outs is not None else spec,
        scratch_shapes=list(scratch),
        compiler_params=pltpu.CompilerParams(vmem_limit_bytes=limit * MIB),
        interpret=INTERPRET,
    )(*args)


def pick(hits, pool):
    hits = hits.astype(bf16)
    high = pool.astype(bf16)
    rest = pool - high.astype(f32)
    mid = rest.astype(bf16)
    low = (rest - mid.astype(f32)).astype(bf16)
    dot = functools.partial(jnp.dot, preferred_element_type=f32)
    return dot(hits, high) + (dot(hits, mid) + dot(hits, low))


def halves(array):
    high = array.astype(bf16)
    return high, (array - high.astype(f32)).astype(bf16)


def product(left, right, dims):
    lh, ll = halves(left)
    rh, rl = halves(right)
    dot = lambda a, b: lax.dot_general(a, b, (dims, ((), ())), preferred_element_type=f32)
    return dot(lh, rh) + (dot(lh, rl) + dot(ll, rh))


def pack_body(jac_hbm, main_ref, rest_ref):
    faces, rows, elems, cols = jac_hbm.shape
    chunk = 27
    extra = cols - LANES

    def step(block, at=None):
        at = (pl.program_id(0) if at is None else at) * chunk
        lane = lax.broadcasted_iota(jnp.int32, (elems, LANES), 1)

        def row(i, _):
            packed = jnp.zeros((elems, LANES), f32)
            for f in range(faces):
                main_ref[f, at + i] = block[f, i, :, 0:LANES]
                tail = jnp.concatenate(
                    [block[f, i, :, LANES:cols], jnp.zeros((elems, LANES - extra), f32)], 1
                )
                if f:
                    tail = pltpu.roll(tail, f * extra, 1)
                packed = packed + tail
            rest_ref[at + i] = packed
            return 0

        lax.fori_loop(0, chunk, row, 0)

    if INTERPRET:
        for c in range(rows // chunk):
            step(jac_hbm[:, c * chunk : (c + 1) * chunk], c)
        return
    pltpu.emit_pipeline(
        step,
        grid=(rows // chunk,),
        in_specs=[pl.BlockSpec((faces, chunk, elems, cols), lambda c: (0, c, 0, 0))],
    )(jac_hbm)


def invert_body(pivot_ref, lower_ref, upper_ref, main_ref, rest_ref, part_ref, wide_ref, side_ref):
    lines, levels, height, _ = main_ref.shape
    cols = part_ref.shape[2]
    extra = cols - LANES
    rows_by_rows = ((1,), (1,))
    rows_by_cols = ((1,), (0,))
    pivot_rows, pair_rows = levels * cols, lines * cols

    def line(l, _):
        wide_ref[0:pivot_rows, :] = pivot_ref[l, :, 0:LANES]
        side_ref[0:pivot_rows, 0:extra] = pivot_ref[l, :, LANES:cols]

        def strided(first, count):
            at = pl.ds(first, cols, stride=count)
            return jnp.concatenate([wide_ref[at, :], side_ref[at, :][:, 0:extra]], 1)

        def pivot_of(k):
            return strided(k, levels)

        def paired(ref, k):
            wide_ref[pivot_rows:, :] = ref[k, :, 0:LANES]
            side_ref[pivot_rows:, 0:extra] = ref[k, :, LANES:cols]
            return strided(pivot_rows + l, lines)

        part_ref[...] = jnp.zeros(part_ref.shape, f32)
        part_ref[0, 0:cols, :] = pivot_of(0).T

        def forward(k, _):
            pivot = pivot_of(k)
            mixed = product(pivot, paired(lower_ref, k - 1), rows_by_cols)
            part_ref[k] = -product(part_ref[k - 1], mixed, rows_by_rows)
            part_ref[k, pl.ds(pl.multiple_of(k * ROWS, 8), cols), :] = pivot.T
            return 0

        lax.fori_loop(1, levels, forward, 0)

        def backward(i, _):
            k = levels - 2 - i
            part_ref[k] = part_ref[k] - product(
                part_ref[k + 1], paired(upper_ref, k), rows_by_rows
            )
            return 0

        lax.fori_loop(0, levels - 1, backward, 0)

        def emit(t, _):
            at = pl.ds(pl.multiple_of(t * ROWS, 8), ROWS)
            packed = jnp.zeros((ROWS, LANES), f32)
            for k in range(levels):
                main_ref[l, k, at, :] = part_ref[k, at, 0:LANES]
                tail = jnp.concatenate(
                    [part_ref[k, at, LANES:cols], jnp.zeros((ROWS, LANES - extra), f32)], 1
                )
                packed = packed + (pltpu.roll(tail, k * extra, 1) if k else tail)
            rest_ref[l, at, :] = packed
            return 0

        lax.fori_loop(0, levels, emit, 0)
        return 0

    lax.fori_loop(0, lines, line, 0)


def solve_body(*refs):
    *blocks, hits_ref, main_ref, rest_ref, out_ref, pool_ref, wide_ref = refs
    lines, levels, height, _ = main_ref.shape
    count = hits_ref.shape[0]
    cols = pool_ref.shape[1]
    extra = cols - LANES
    fill_pool(blocks, pool_ref)
    rhs = pick(hits_ref[...], pool_ref[...])
    rhs = jnp.concatenate([rhs, jnp.zeros((count, 2 * LANES - cols), f32)], 1)
    rhs = rhs.T[0:ROWS]
    for q in range(count):
        wide_ref[q] = jnp.broadcast_to(rhs[:, q : q + 1], (ROWS, LANES))
    for l in range(lines):

        def member(m, sums):
            sums = list(sums)
            for t in range(ROWS // 8):
                at = pl.ds(pl.multiple_of(m * ROWS + t * 8, 8), 8)
                value = wide_ref[l * levels + m, t * 8 : t * 8 + 8, :]
                for k in range(levels):
                    sums[k] = sums[k] + main_ref[l, k, at, :] * value
                sums[levels] = sums[levels] + rest_ref[l, at, :] * value
            return tuple(sums)

        zero = jnp.zeros((8, LANES), f32)
        sums = lax.fori_loop(0, levels, member, (zero,) * (levels + 1))
        tails = jnp.sum(sums[levels], axis=0, keepdims=True)
        tails = jnp.broadcast_to(tails, (8, LANES))
        for k in range(levels):
            at = slice(l * levels + k, l * levels + k + 1)
            out_ref[at, 0:LANES] = jnp.sum(sums[k], axis=0, keepdims=True)
            tail = pltpu.roll(tails, LANES - k * extra, 1) if k else tails
            out_ref[at, LANES:cols] = tail[0:1, 0:extra]


def fill_pool(blocks, pool_ref):
    at = 0
    for block in blocks:
        count = block.shape[0]
        pool_ref[at : at + count, :] = block[...]
        at += count


def operate(blocks, hits_ref, main_ref, rest_ref, pool_ref):
    faces, rows, elems, _ = main_ref.shape
    cols = pool_ref.shape[1]
    extra = cols - LANES
    fill_pool(blocks, pool_ref)
    field = pick(hits_ref[...], pool_ref[...])
    heads = [field[f * elems : (f + 1) * elems, 0:LANES] for f in range(faces)]
    packed = jnp.zeros((elems, LANES), f32)
    for f in range(faces):
        tail = jnp.concatenate(
            [field[f * elems : (f + 1) * elems, LANES:cols], jnp.zeros((elems, LANES - extra), f32)], 1
        )
        packed = packed + (pltpu.roll(tail, f * extra, 1) if f else tail)
    lane = lax.broadcasted_iota(jnp.int32, (elems, LANES), 1)

    def one(i):
        total = rest_ref[i] * packed
        for f in range(faces):
            total = total + main_ref[f, i] * heads[f]
        return jnp.sum(total, axis=1, keepdims=True)

    group = 16

    def some(g, image):
        for s in range(group):
            i = g * group + s
            image = jnp.where(lane == i, one(i), image)
        return image

    image = lax.fori_loop(0, LANES // group, some, jnp.zeros((elems, LANES), f32))
    tail = jnp.zeros((elems, LANES), f32)
    for c in range(extra):
        tail = jnp.where(lane == c, one(LANES + c), tail)
    return jnp.concatenate([image, tail[:, 0:extra]], 1)


def row_of(values):
    lane = lax.broadcasted_iota(jnp.int32, (1, LANES), 1)
    row = jnp.zeros((1, LANES), f32)
    for i, value in values.items():
        total = jnp.sum(jnp.sum(value, axis=0, keepdims=True), axis=1, keepdims=True)
        row = jnp.where(lane == i, total, row)
    return row


def lane_of(row, i):
    return row[:, i : i + 1]


UC, UU, CC = 13, 14, 15
SHIFT, SCALE, STEP = 0, 1, 2


def totals(parts_ref):
    return jnp.sum(parts_ref[...], axis=0, keepdims=True)


def project_body(images_ref, residual_ref, out_ref):
    residual = residual_ref[...]
    out_ref[...] = row_of({k: images_ref[k] * residual for k in range(images_ref.shape[0])})


def deflate_body(entries, parts_ref, residual_ref, basis_ref, images_ref, correction_ref, start_ref):
    row = totals(parts_ref) / entries
    correction = jnp.zeros(residual_ref.shape, f32)
    start = residual_ref[...]
    for k in range(basis_ref.shape[0]):
        weight = lane_of(row, k)
        correction = correction + weight * basis_ref[k]
        start = start - weight * images_ref[k]
    correction_ref[...] = correction
    start_ref[...] = start


def first_body(*refs):
    *blocks, u_ref, hits_ref, main_ref, rest_ref, c_ref, part_ref, pool_ref = refs
    c = operate(blocks, hits_ref, main_ref, rest_ref, pool_ref)
    c_ref[...] = c
    u = u_ref[...]
    part_ref[...] = row_of({UC: u * c, UU: u * u, CC: c * c})


def advance(entries, row, u, c, known, basis):
    scale, step = lane_of(known, SCALE), lane_of(known, STEP)
    norm = jnp.sqrt(lane_of(row, UU) / entries + EPS / (scale * scale))
    inverse = 1.0 / norm
    here = u * inverse
    image = c * inverse
    lane = lax.broadcasted_iota(jnp.int32, (1, LANES), 1)
    own = lane_of(row, UC) * inverse * inverse / entries
    column = jnp.where(lane < STEPS, row * inverse / entries, 0.0)
    column = jnp.where(lane.astype(f32) == step, own, column)
    scale_next = jnp.sqrt(lane_of(row, CC) * inverse * inverse / entries + EPS)
    reduced = image - own * here
    for i in range(STEPS):
        reduced = reduced - lane_of(row, i) * inverse / entries * basis[i]
    return here, image, inverse, own, column, scale * norm, reduced / scale_next, scale_next


def place(out_ref, in_ref, step, value):
    for i in range(in_ref.shape[0]):
        out_ref[i] = jnp.where(step == i, value, in_ref[i])


def record(hess_out, hess_ref, step, column, below):
    at = lax.broadcasted_iota(jnp.int32, hess_ref.shape, 0).astype(f32)
    lane = lax.broadcasted_iota(jnp.int32, hess_ref.shape, 1).astype(f32)
    hess = jnp.where(at == step, column, hess_ref[...])
    hess_out[...] = jnp.where((at == STEPS) & (lane == step), below, hess)


def numbers(shift, scale, step):
    lane = lax.broadcasted_iota(jnp.int32, (1, LANES), 1)
    row = jnp.where(lane == SHIFT, shift, jnp.zeros((1, LANES), f32))
    row = jnp.where(lane == SCALE, scale, row)
    return jnp.where(lane == STEP, step, row)


def next_body(entries, *refs):
    *blocks, hits_ref, main_ref, rest_ref, sums_ref, u_ref, c_ref, known_ref = refs[:-12]
    basis_ref, images_ref, hess_ref, basis_out, images_out, hess_out = refs[-12:-6]
    u_out, c_out, v_out, known_out, part_ref, pool_ref = refs[-6:]
    w = operate(blocks, hits_ref, main_ref, rest_ref, pool_ref)
    known = known_ref[...]
    step = lane_of(known, STEP)
    row = totals(sums_ref)
    here, image, inverse, own, column, below, u, scale = advance(
        entries, row, u_ref[...], c_ref[...], known, basis_ref
    )
    moved = w * inverse - (own - lane_of(known, SHIFT)) * image
    for i in range(STEPS):
        moved = moved - lane_of(row, i) * inverse / entries * images_ref[i]
    c = moved / scale
    place(basis_out, basis_ref, step, here)
    place(images_out, images_ref, step, image)
    record(hess_out, hess_ref, step, column, below)
    u_out[...] = u
    c_out[...] = c
    v_out[...] = c - own * u
    known_out[...] = numbers(own, scale, step + 1.0)
    products = {i: jnp.where(step == i, here, basis_ref[i]) * c for i in range(STEPS)}
    products.update({UC: u * c, UU: u * u, CC: c * c})
    part_ref[...] = row_of(products)


def last_body(entries, sums_ref, u_ref, c_ref, known_ref, basis_ref, hess_ref, *outs):
    basis_out, hess_out, u_out, known_out, part_ref = outs
    known = known_ref[...]
    step = lane_of(known, STEP)
    here, _, _, own, column, below, u, scale = advance(
        entries, totals(sums_ref), u_ref[...], c_ref[...], known, basis_ref
    )
    place(basis_out, basis_ref, step, here)
    record(hess_out, hess_ref, step, column, below)
    u_out[...] = u
    known_out[...] = numbers(own, scale, step + 1.0)
    part_ref[...] = row_of({UU: u * u})


def finish_body(entries, sums_ref, u_ref, known_ref, basis_ref, hess_ref, basis_out, hess_out, norm_ref):
    scale = lane_of(known_ref[...], SCALE)
    norm = jnp.sqrt(lane_of(totals(sums_ref), UU) / entries + EPS / (scale * scale))
    for i in range(STEPS):
        basis_out[i] = basis_ref[i]
    basis_out[STEPS] = u_ref[...] / norm
    lane = lax.broadcasted_iota(jnp.int32, (1, LANES), 1)
    norms = hess_ref[STEPS : STEPS + 1, :]
    for j in range(STEPS):
        below = lane_of(norms, j + 1) if j + 1 < STEPS else scale * norm
        hess_out[j : j + 1, :] = jnp.where(lane == j + 1, below, hess_ref[j : j + 1, :])
    norm_ref[...] = norms


def shifted(array, d_dom, d_blk):
    doms, blks = lax.axis_size("dom"), lax.axis_size("blk")
    if d_dom == 0 and d_blk == 0:
        return array
    pairs = []
    for d in range(doms):
        for b in range(blks):
            source = ((d + d_dom) % doms) * blks + (b + d_blk) % blks
            pairs.append((source, d * blks + b))
    return lax.ppermute(array, ("dom", "blk"), pairs)


def partition(array):
    return [shifted(array, 0, b) for b in range(lax.axis_size("blk"))]


def near_rows(array):
    blks = lax.axis_size("blk")
    return [shifted(array, d, b) for d in (-1, 0, 1) for b in range(blks)]


def far_rows(array):
    whole = jnp.concatenate(partition(array), 0)
    return [shifted(whole, d, 0) for d in (-2, -1, 0, 1, 2)]


def gathered(part):
    return lax.all_gather(part, ("dom", "blk"), axis=0, tiled=True)


def added(part):
    doms, blks = lax.axis_size("dom"), lax.axis_size("blk")
    devices = doms * blks
    reach = 1
    while reach < devices:
        ways = 4 if reach * 4 <= devices else 2
        others = [
            lax.ppermute(part, ("dom", "blk"), [(n ^ (k * reach), n) for n in range(devices)])
            for k in range(1, ways)
        ]
        if ways == 4:
            part = (part + others[0]) + (others[1] + others[2])
        else:
            part = part + others[0]
        reach *= ways
    return part


def per_device(residual, recycle_basis, recycle_images, jacobian, neighbours, line_members,
               line_pivots, line_lower, line_upper):
    elems, cols = residual.shape
    doms, blks = lax.axis_size("dom"), lax.axis_size("blk")
    faces = jacobian.shape[1]
    lines, levels = line_pivots.shape[:2]
    entries = float(elems * cols * doms * blks)
    dom, blk = lax.axis_index("dom"), lax.axis_index("blk")
    devices = doms * blks

    row = jax.ShapeDtypeStruct((1, LANES), f32)
    rows = jax.ShapeDtypeStruct((elems, cols), f32)
    projected = added(call(project_body, row, recycle_images, residual))

    members = line_members.reshape(devices, elems)
    near = jnp.array([(d, b) for d in range(-2, 3) for b in range(blks)], jnp.int32)
    at = (dom + near[:, 0] + doms) % doms * blks + (blk + near[:, 1]) % blks
    line_ids = members[at].reshape(-1)
    near_own = at[blks : 4 * blks]
    elem_ids = (near_own[:, None] * elems + jnp.arange(elems, dtype=jnp.int32)).reshape(-1)
    me = dom * blks + blk
    own_ids = me * elems + jnp.arange(elems, dtype=jnp.int32)
    wanted = jnp.concatenate([own_ids[None], neighbours.T], 0).reshape(-1)
    stencil = (wanted[:, None] == line_ids[None, :]).astype(f32)
    mine = lax.dynamic_slice_in_dim(members, me, 1, 0)[0]
    entering = (mine[:, None] == elem_ids[None, :]).astype(f32)

    spec = pl.BlockSpec(memory_space=pltpu.VMEM)
    hbm = pl.BlockSpec(memory_space=pl.ANY)
    jac = jnp.transpose(jacobian, (1, 2, 0, 3))
    jac_main, jac_rest = call(
        pack_body,
        [vmem_out((faces, cols, elems, LANES)), vmem_out((cols, elems, LANES))],
        jac,
        specs=[spec if INTERPRET else hbm],
        limit=24,
    )
    pivots = jnp.transpose(line_pivots, (0, 2, 1, 3)).reshape(lines, cols * levels, cols)
    lower = jnp.transpose(line_lower, (1, 2, 0, 3)).reshape(levels - 1, cols * lines, cols)
    upper = jnp.transpose(line_upper, (1, 2, 0, 3)).reshape(levels - 1, cols * lines, cols)
    height = levels * ROWS
    inv_main, inv_rest = call(
        invert_body,
        [vmem_out((lines, levels, height, LANES)), vmem_out((lines, height, LANES))],
        pivots,
        lower,
        upper,
        scratch=[
            pltpu.VMEM((levels, height, cols), f32),
            pltpu.VMEM(((levels + lines) * cols, LANES), f32),
            pltpu.VMEM(((levels + lines) * cols, LANES), f32),
        ],
        limit=40,
    )
    jac_main, jac_rest, inv_main, inv_rest = map(in_vmem, (jac_main, jac_rest, inv_main, inv_rest))

    correction, u = call(
        functools.partial(deflate_body, entries),
        [rows, rows],
        projected,
        residual,
        recycle_basis,
        recycle_images,
    )

    def precondition(v):
        z = call(
            solve_body,
            rows,
            *near_rows(v),
            entering,
            inv_main,
            inv_rest,
            scratch=[
                pltpu.VMEM((entering.shape[1], cols), f32),
                pltpu.VMEM((elems, ROWS, LANES), f32),
            ],
        )
        return far_rows(z)

    stencil_pool = pltpu.VMEM((stencil.shape[1], cols), f32)
    matrices = (stencil, jac_main, jac_rest)
    c, part = call(
        first_body, [rows, row], *precondition(u), u, *matrices, scratch=[stencil_pool]
    )
    stack = jax.ShapeDtypeStruct((STEPS, elems, cols), f32)
    hess = jax.ShapeDtypeStruct((2 * STEPS, LANES), f32)

    def step(_, state):
        basis, images, hessenberg, u, c, v, known, part = state
        return tuple(
            call(
                functools.partial(next_body, entries),
                [stack, stack, hess, rows, rows, rows, row, row],
                *precondition(v),
                *matrices,
                gathered(part),
                u,
                c,
                known,
                basis,
                images,
                hessenberg,
                scratch=[stencil_pool],
            )
        )

    empty = jnp.zeros(stack.shape, f32)
    known = jnp.zeros((1, LANES), f32).at[0, SCALE].set(1.0)
    state = (empty, empty, jnp.zeros(hess.shape, f32), u, c, c, known, part)
    basis, _, hessenberg, u, c, _, known, part = lax.fori_loop(0, STEPS - 1, step, state)
    basis, hessenberg, u, known, part = call(
        functools.partial(last_body, entries),
        [stack, hess, rows, row, row],
        added(part),
        u,
        c,
        known,
        basis,
        hessenberg,
    )
    basis, hessenberg, norm = call(
        functools.partial(finish_body, entries),
        [
            jax.ShapeDtypeStruct((STEPS + 1, elems, cols), f32),
            jax.ShapeDtypeStruct((STEPS, LANES), f32),
            row,
        ],
        added(part),
        u,
        known,
        basis,
        hessenberg,
    )
    return correction, basis, hessenberg[:, : STEPS + 1].T, norm[0, 0]


def solution(mesh):
    both = ("dom", "blk")
    in_specs = (
        P(both, None),
        P(None, both, None),
        P(None, both, None),
        P(both, None, None, None),
        P(both, None),
        P(),
        P(both, None, None, None),
        P(both, None, None, None),
        P(both, None, None, None),
    )
    out_specs = (P(both, None), P(None, both, None), P(), P())
    return jax.shard_map(
        per_device, mesh=mesh, in_specs=in_specs, out_specs=out_specs, check_vma=False
    )
```

```python
import functools

import jax
import jax.numpy as jnp
from jax import lax
from jax.experimental import pallas as pl
from jax.experimental.pallas import tpu as pltpu
from jax.sharding import PartitionSpec as P

STEPS = 8
EPS = 1e-06
KEPT = 2e-3
SAMPLE = 16
LANES = 128
ROWS = 136
INTERPRET = False
f32 = jnp.float32
bf16 = jnp.bfloat16
MIB = 1024 * 1024


def vmem_out(shape):
    if INTERPRET:
        return jax.ShapeDtypeStruct(shape, f32)
    return pltpu.VMEM(shape, f32)


def in_vmem(array):
    return array if INTERPRET else pltpu.with_memory_space_constraint(array, pltpu.VMEM)


def in_hbm(array):
    return array if INTERPRET else pltpu.with_memory_space_constraint(array, pltpu.HBM)


def call(body, out_shape, *args, scratch=(), limit=24, specs=None):
    spec = pl.BlockSpec(memory_space=pltpu.VMEM)
    outs = out_shape if isinstance(out_shape, (list, tuple)) else None
    return pl.pallas_call(
        body,
        out_shape=out_shape,
        in_specs=specs if specs is not None else [spec] * len(args),
        out_specs=[spec] * len(outs) if outs is not None else spec,
        scratch_shapes=list(scratch),
        compiler_params=pltpu.CompilerParams(vmem_limit_bytes=limit * MIB),
        interpret=INTERPRET,
    )(*args)


def pick(hits, pool):
    hits = hits.astype(bf16)
    high = pool.astype(bf16)
    rest = pool - high.astype(f32)
    mid = rest.astype(bf16)
    low = (rest - mid.astype(f32)).astype(bf16)
    dot = functools.partial(jnp.dot, preferred_element_type=f32)
    return dot(hits, high) + (dot(hits, mid) + dot(hits, low))


def halves(array):
    high = array.astype(bf16)
    return high, (array - high.astype(f32)).astype(bf16)


def product(left, right, dims):
    lh, ll = halves(left)
    rh, rl = halves(right)
    dot = lambda a, b: lax.dot_general(a, b, (dims, ((), ())), preferred_element_type=f32)
    return dot(lh, rh) + (dot(lh, rl) + dot(ll, rh))


def pack_body(jac_hbm, main_ref, rest_ref, token_ref):
    faces, rows, elems, cols = jac_hbm.shape
    chunk, group = 27, 9
    token_ref[...] = jnp.zeros(token_ref.shape, f32)
    extra = cols - LANES

    def step(block, at=None):
        at = (pl.program_id(0) if at is None else at) * chunk
        lane = lax.broadcasted_iota(jnp.int32, (elems, LANES), 1)

        def row(i):
            packed = jnp.zeros((elems, LANES), f32)
            for f in range(faces):
                main_ref[f, at + i] = block[f, i, :, 0:LANES]
                tail = jnp.concatenate(
                    [block[f, i, :, LANES:cols], jnp.zeros((elems, LANES - extra), f32)], 1
                )
                if f:
                    tail = pltpu.roll(tail, f * extra, 1)
                packed = packed + tail
            rest_ref[at + i] = packed

        def some(g, _):
            for n in range(group):
                row(g * group + n)
            return 0

        lax.fori_loop(0, chunk // group, some, 0)

    if INTERPRET:
        for c in range(rows // chunk):
            step(jac_hbm[:, c * chunk : (c + 1) * chunk], c)
        return
    pltpu.emit_pipeline(
        step,
        grid=(rows // chunk,),
        in_specs=[pl.BlockSpec((faces, chunk, elems, cols), lambda c: (0, c, 0, 0))],
    )(jac_hbm)


def invert_body(l, lines, pivot_ref, lower_ref, upper_ref, main_ref, rest_ref, token_ref, part_ref, wide_ref, side_ref):
    levels, height, _ = main_ref.shape
    cols = part_ref.shape[2]
    extra = cols - LANES
    rows_by_rows = ((1,), (1,))
    rows_by_cols = ((1,), (0,))
    pivot_rows = levels * cols
    token_ref[...] = jnp.zeros(token_ref.shape, f32)
    wide_ref[0:pivot_rows, :] = pivot_ref[l, :, 0:LANES]
    side_ref[0:pivot_rows, 0:extra] = pivot_ref[l, :, LANES:cols]

    def strided(first, count):
        at = pl.ds(first, cols, stride=count)
        return jnp.concatenate([wide_ref[at, :], side_ref[at, :][:, 0:extra]], 1)

    def paired(ref, k):
        wide_ref[pivot_rows:, :] = ref[k, :, 0:LANES]
        side_ref[pivot_rows:, 0:extra] = ref[k, :, LANES:cols]
        return strided(pivot_rows + l, lines)

    part_ref[...] = jnp.zeros(part_ref.shape, f32)
    part_ref[0, 0:cols, :] = strided(0, levels).T
    for k in range(1, levels):
        pivot = strided(k, levels)
        mixed = product(pivot, paired(lower_ref, k - 1), rows_by_cols)
        before = part_ref[k - 1, 0 : k * ROWS, :]
        part_ref[k, 0 : k * ROWS, :] = -product(before, mixed, rows_by_rows)
        part_ref[k, k * ROWS : k * ROWS + cols, :] = pivot.T

    def backward(i, _):
        k = levels - 2 - i
        part_ref[k] = part_ref[k] - product(part_ref[k + 1], paired(upper_ref, k), rows_by_rows)
        return 0

    lax.fori_loop(0, levels - 1, backward, 0)

    def emit(t, _):
        at = pl.ds(pl.multiple_of(t * ROWS, 8), ROWS)
        packed = jnp.zeros((ROWS, LANES), f32)
        for k in range(levels):
            main_ref[k, at, :] = part_ref[k, at, 0:LANES]
            tail = jnp.concatenate(
                [part_ref[k, at, LANES:cols], jnp.zeros((ROWS, LANES - extra), f32)], 1
            )
            packed = packed + (pltpu.roll(tail, k * extra, 1) if k else tail)
        rest_ref[at, :] = packed
        return 0

    lax.fori_loop(0, levels, emit, 0)


def solve_body(lines, *refs):
    blocks, refs = refs[: -4 - 2 * lines], refs[-4 - 2 * lines :]
    hits_ref, out_ref, pool_ref, wide_ref = refs[0], *refs[-3:]
    mains, rests = refs[1 : 1 + lines], refs[1 + lines : 1 + 2 * lines]
    levels = mains[0].shape[0]
    count = hits_ref.shape[0]
    cols = pool_ref.shape[1]
    extra = cols - LANES
    fill_pool(blocks, pool_ref)
    rhs = pick(hits_ref[...], pool_ref[...])
    rhs = jnp.concatenate([rhs, jnp.zeros((count, 2 * LANES - cols), f32)], 1)
    rhs = rhs.T[0:ROWS]
    for q in range(count):
        wide_ref[q] = jnp.broadcast_to(rhs[:, q : q + 1], (ROWS, LANES))
    for l in range(lines):

        def member(m, sums):
            sums = list(sums)
            for t in range(ROWS // 8):
                at = pl.ds(pl.multiple_of(m * ROWS + t * 8, 8), 8)
                value = wide_ref[l * levels + m, t * 8 : t * 8 + 8, :]
                for k in range(levels):
                    sums[k] = sums[k] + mains[l][k, at, :] * value
                sums[levels] = sums[levels] + rests[l][at, :] * value
            return tuple(sums)

        zero = jnp.zeros((8, LANES), f32)
        sums = lax.fori_loop(0, levels, member, (zero,) * (levels + 1))
        tails = jnp.sum(sums[levels], axis=0, keepdims=True)
        tails = jnp.broadcast_to(tails, (8, LANES))
        for k in range(levels):
            at = slice(l * levels + k, l * levels + k + 1)
            out_ref[at, 0:LANES] = jnp.sum(sums[k], axis=0, keepdims=True)
            tail = pltpu.roll(tails, LANES - k * extra, 1) if k else tails
            out_ref[at, LANES:cols] = tail[0:1, 0:extra]


def fill_pool(blocks, pool_ref):
    at = 0
    for block in blocks:
        count = block.shape[0]
        pool_ref[at : at + count, :] = block[...]
        at += count


def operate(blocks, hits_ref, main_ref, rest_ref, pool_ref):
    faces, rows, elems, _ = main_ref.shape
    cols = pool_ref.shape[1]
    extra = cols - LANES
    fill_pool(blocks, pool_ref)
    field = pick(hits_ref[...], pool_ref[...])
    heads = [field[f * elems : (f + 1) * elems, 0:LANES] for f in range(faces)]
    packed = jnp.zeros((elems, LANES), f32)
    for f in range(faces):
        tail = jnp.concatenate(
            [field[f * elems : (f + 1) * elems, LANES:cols], jnp.zeros((elems, LANES - extra), f32)], 1
        )
        packed = packed + (pltpu.roll(tail, f * extra, 1) if f else tail)
    lane = lax.broadcasted_iota(jnp.int32, (elems, LANES), 1)

    def one(i):
        total = rest_ref[i] * packed
        for f in range(faces):
            total = total + main_ref[f, i] * heads[f]
        return jnp.sum(total, axis=1, keepdims=True)

    group = 16

    def some(g, image):
        for s in range(group):
            i = g * group + s
            image = jnp.where(lane == i, one(i), image)
        return image

    image = lax.fori_loop(0, LANES // group, some, jnp.zeros((elems, LANES), f32))
    tail = jnp.zeros((elems, LANES), f32)
    for c in range(extra):
        tail = jnp.where(lane == c, one(LANES + c), tail)
    return jnp.concatenate([image, tail[:, 0:extra]], 1)


def row_of(values):
    lane = lax.broadcasted_iota(jnp.int32, (1, LANES), 1)
    row = jnp.zeros((1, LANES), f32)
    for i, value in values.items():
        total = jnp.sum(jnp.sum(value, axis=0, keepdims=True), axis=1, keepdims=True)
        row = jnp.where(lane == i, total, row)
    return row


def lane_of(row, i):
    return row[:, i : i + 1]


UC, UU, CC = 13, 14, 15
SHIFT, SCALE, STEP = 0, 1, 2


def totals(parts_ref):
    return jnp.sum(parts_ref[...], axis=0, keepdims=True)


def project_body(images_ref, residual_ref, jac_ref, pivot_ref, out_ref):
    residual = residual_ref[...]
    products = {k: images_ref[k] * residual for k in range(STEPS)}
    lane = lax.broadcasted_iota(jnp.int32, jac_ref.shape[1:], 1)
    own = jnp.zeros(jac_ref.shape[1:], f32)
    for i in range(SAMPLE):
        own = jnp.where(lane == i, jac_ref[i], own)
    products[STEPS] = own
    lines, _, levels, _ = pivot_ref.shape
    lane = lax.broadcasted_iota(jnp.int32, pivot_ref.shape[2:], 1)
    own = jnp.zeros(pivot_ref.shape[2:], f32)
    for l in range(lines):
        for i in range(SAMPLE):
            own = own + jnp.where(lane == i, pivot_ref[l, i], 0.0)
    products[STEPS + 1] = own
    out_ref[...] = row_of(products)


def deflate_body(entries, parts_ref, residual_ref, basis_ref, images_ref, correction_ref, start_ref):
    row = totals(parts_ref) / entries
    correction = jnp.zeros(residual_ref.shape, f32)
    start = residual_ref[...]
    for k in range(basis_ref.shape[0]):
        weight = lane_of(row, k)
        correction = correction + weight * basis_ref[k]
        start = start - weight * images_ref[k]
    correction_ref[...] = correction
    start_ref[...] = start


def shift_of(row, count):
    return lane_of(row, STEPS) / count * (lane_of(row, STEPS + 1) / count)


def power_body(count, *refs):
    *blocks, u_ref, row_ref, hits_ref, main_ref, rest_ref, out_ref, pool_ref = refs
    image = operate(blocks, hits_ref, main_ref, rest_ref, pool_ref)
    out_ref[...] = image - shift_of(row_ref[...], count) * u_ref[...]


def power_last_body(count, *refs):
    blocks, vectors, refs = refs[: -8 - STEPS], refs[-8 - STEPS : -8], refs[-8:]
    u_ref, row_ref, hits_ref, main_ref, rest_ref, out_ref, part_ref, pool_ref = refs
    image = operate(blocks, hits_ref, main_ref, rest_ref, pool_ref)
    last = image - shift_of(row_ref[...], count) * u_ref[...]
    out_ref[...] = last
    vectors = [v[...] for v in vectors] + [last]
    at = lax.broadcasted_iota(jnp.int32, part_ref.shape, 0)
    lane = lax.broadcasted_iota(jnp.int32, part_ref.shape, 1)
    part = jnp.zeros(part_ref.shape, f32)
    for k, right in enumerate(vectors):
        for i in range(k + 1):
            total = jnp.sum(vectors[i] * right, axis=0, keepdims=True)
            total = jnp.sum(total, axis=1, keepdims=True)
            here = ((at == i) & (lane == k)) | ((at == k) & (lane == i))
            part = jnp.where(here, total, part)
    part_ref[...] = part


def combine_body(entries, count, *refs):
    gram_ref, row_ref, *vectors = refs[: 3 + STEPS]
    basis_out, hess_out, norm_ref, sure_ref = refs[3 + STEPS :]
    shift = shift_of(row_ref[...], count)
    gram = gram_ref[...] / entries
    size = jnp.abs(gram)
    at = lax.broadcasted_iota(jnp.int32, gram.shape, 0)
    lane = lax.broadcasted_iota(jnp.int32, gram.shape, 1)

    def across(values):
        return jnp.sum(values, axis=1, keepdims=True)

    def turned(column):
        return jnp.sum(jnp.where(at == lane, column, 0.0), axis=0, keepdims=True)

    def times(matrix, row):
        return turned(across(matrix * row))

    first = lane[0:1]
    norm = jnp.sqrt(gram[0:1, 0:1] + EPS)
    norm_ref[...] = jnp.broadcast_to(norm, (1, LANES))
    newest = jnp.where(first == 0, 1.0 / norm, 0.0)
    known = jnp.where(at == 0, newest, 0.0)
    sure = jnp.full((1, 1), 1.0, f32)
    for j in range(STEPS):
        moved = pltpu.roll(jnp.broadcast_to(newest, (8, LANES)), 1, 1)[0:1]
        image = moved + shift * newest
        inner = across(known * times(gram, image))
        reduced = image - jnp.sum(known * inner, axis=0, keepdims=True)
        square = across(reduced * times(gram, reduced))
        terms = across(jnp.abs(reduced) * times(size, jnp.abs(reduced)))
        sure = jnp.where(square > KEPT * terms, sure, 0.0)
        below = jnp.sqrt(jnp.maximum(square, 0.0) + EPS)
        column = jnp.where(first <= j, turned(inner), 0.0)
        hess_out[j : j + 1, :] = jnp.where(first == j + 1, below, column)
        newest = reduced / below
        known = jnp.where(at == j + 1, newest, known)
    sure_ref[...] = jnp.broadcast_to(sure, (1, LANES))
    vectors = [v[...] for v in vectors]
    for j in range(STEPS + 1):
        value = known[j : j + 1, 0:1] * vectors[0]
        for k in range(1, j + 1):
            value = value + known[j : j + 1, k : k + 1] * vectors[k]
        basis_out[j] = value


def first_body(*refs):
    *blocks, u_ref, hits_ref, main_ref, rest_ref, c_ref, part_ref, pool_ref = refs
    c = operate(blocks, hits_ref, main_ref, rest_ref, pool_ref)
    c_ref[...] = c
    u = u_ref[...]
    part_ref[...] = row_of({UC: u * c, UU: u * u, CC: c * c})


def advance(entries, row, u, c, known, basis):
    scale, step = lane_of(known, SCALE), lane_of(known, STEP)
    norm = jnp.sqrt(lane_of(row, UU) / entries + EPS / (scale * scale))
    inverse = 1.0 / norm
    here = u * inverse
    image = c * inverse
    lane = lax.broadcasted_iota(jnp.int32, (1, LANES), 1)
    own = lane_of(row, UC) * inverse * inverse / entries
    column = jnp.where(lane < STEPS, row * inverse / entries, 0.0)
    column = jnp.where(lane.astype(f32) == step, own, column)
    scale_next = jnp.sqrt(lane_of(row, CC) * inverse * inverse / entries + EPS)
    reduced = image - own * here
    for i in range(STEPS):
        reduced = reduced - lane_of(row, i) * inverse / entries * basis[i]
    return here, image, inverse, own, column, scale * norm, reduced / scale_next, scale_next


def place(out_ref, in_ref, step, value):
    for i in range(in_ref.shape[0]):
        out_ref[i] = jnp.where(step == i, value, in_ref[i])


def record(hess_out, hess_ref, step, column, below):
    at = lax.broadcasted_iota(jnp.int32, hess_ref.shape, 0).astype(f32)
    lane = lax.broadcasted_iota(jnp.int32, hess_ref.shape, 1).astype(f32)
    hess = jnp.where(at == step, column, hess_ref[...])
    hess_out[...] = jnp.where((at == STEPS) & (lane == step), below, hess)


def numbers(shift, scale, step):
    lane = lax.broadcasted_iota(jnp.int32, (1, LANES), 1)
    row = jnp.where(lane == SHIFT, shift, jnp.zeros((1, LANES), f32))
    row = jnp.where(lane == SCALE, scale, row)
    return jnp.where(lane == STEP, step, row)


def next_body(entries, *refs):
    *blocks, hits_ref, main_ref, rest_ref, sums_ref, u_ref, c_ref, known_ref = refs[:-12]
    basis_ref, images_ref, hess_ref, basis_out, images_out, hess_out = refs[-12:-6]
    u_out, c_out, v_out, known_out, part_ref, pool_ref = refs[-6:]
    w = operate(blocks, hits_ref, main_ref, rest_ref, pool_ref)
    known = known_ref[...]
    step = lane_of(known, STEP)
    row = totals(sums_ref)
    here, image, inverse, own, column, below, u, scale = advance(
        entries, row, u_ref[...], c_ref[...], known, basis_ref
    )
    moved = w * inverse - (own - lane_of(known, SHIFT)) * image
    for i in range(STEPS):
        moved = moved - lane_of(row, i) * inverse / entries * images_ref[i]
    c = moved / scale
    place(basis_out, basis_ref, step, here)
    place(images_out, images_ref, step, image)
    record(hess_out, hess_ref, step, column, below)
    u_out[...] = u
    c_out[...] = c
    v_out[...] = c - own * u
    known_out[...] = numbers(own, scale, step + 1.0)
    products = {i: jnp.where(step == i, here, basis_ref[i]) * c for i in range(STEPS)}
    products.update({UC: u * c, UU: u * u, CC: c * c})
    part_ref[...] = row_of(products)


def last_body(entries, sums_ref, u_ref, c_ref, known_ref, basis_ref, hess_ref, *outs):
    basis_out, hess_out, u_out, known_out, part_ref = outs
    known = known_ref[...]
    step = lane_of(known, STEP)
    here, _, _, own, column, below, u, scale = advance(
        entries, totals(sums_ref), u_ref[...], c_ref[...], known, basis_ref
    )
    place(basis_out, basis_ref, step, here)
    record(hess_out, hess_ref, step, column, below)
    u_out[...] = u
    known_out[...] = numbers(own, scale, step + 1.0)
    part_ref[...] = row_of({UU: u * u})


def finish_body(entries, sums_ref, u_ref, known_ref, basis_ref, hess_ref, basis_out, hess_out, norm_ref):
    scale = lane_of(known_ref[...], SCALE)
    norm = jnp.sqrt(lane_of(totals(sums_ref), UU) / entries + EPS / (scale * scale))
    for i in range(STEPS):
        basis_out[i] = basis_ref[i]
    basis_out[STEPS] = u_ref[...] / norm
    lane = lax.broadcasted_iota(jnp.int32, (1, LANES), 1)
    norms = hess_ref[STEPS : STEPS + 1, :]
    for j in range(STEPS):
        below = lane_of(norms, j + 1) if j + 1 < STEPS else scale * norm
        hess_out[j : j + 1, :] = jnp.where(lane == j + 1, below, hess_ref[j : j + 1, :])
    norm_ref[...] = norms


def shifted(array, d_dom, d_blk):
    doms, blks = lax.axis_size("dom"), lax.axis_size("blk")
    if d_dom == 0 and d_blk == 0:
        return array
    pairs = []
    for d in range(doms):
        for b in range(blks):
            source = ((d + d_dom) % doms) * blks + (b + d_blk) % blks
            pairs.append((source, d * blks + b))
    return lax.ppermute(array, ("dom", "blk"), pairs)


def around(array, reach):
    blks = lax.axis_size("blk")
    whole = jnp.concatenate([shifted(array, 0, b) for b in range(blks)], 0)
    return [shifted(whole, d, 0) for d in range(-reach, reach + 1)]


def added(part, beside=()):
    beside = list(beside)
    doms, blks = lax.axis_size("dom"), lax.axis_size("blk")
    devices = doms * blks
    reach = 1
    while reach < devices:
        ways = 4 if reach * 4 <= devices else 2
        others = [
            lax.ppermute(part, ("dom", "blk"), [(n ^ (k * reach), n) for n in range(devices)])
            for k in range(1, ways)
        ]
        if ways == 4:
            part = (part + others[0]) + (others[1] + others[2])
        else:
            part = part + others[0]
        if beside:
            part = part + beside.pop(0)()
        reach *= ways
    return part


def matrices_of(jacobian, line_pivots, line_lower, line_upper):
    elems, faces, cols, _ = jacobian.shape
    lines, levels = line_pivots.shape[:2]
    height = levels * ROWS
    token = jax.ShapeDtypeStruct((1, LANES), f32)
    kept = {}

    def pack():
        main, rest, done = call(
            pack_body,
            [vmem_out((faces, cols, elems, LANES)), vmem_out((cols, elems, LANES)), token],
            in_hbm(jnp.transpose(jacobian, (1, 2, 0, 3))),
            specs=[pl.BlockSpec(memory_space=pltpu.VMEM if INTERPRET else pltpu.HBM)],
            limit=16,
        )
        kept["jac"] = in_vmem(main), in_vmem(rest)
        return done

    pivots = jnp.transpose(line_pivots, (0, 2, 1, 3)).reshape(lines, cols * levels, cols)
    lower = jnp.transpose(line_lower, (1, 2, 0, 3)).reshape(levels - 1, cols * lines, cols)
    upper = jnp.transpose(line_upper, (1, 2, 0, 3)).reshape(levels - 1, cols * lines, cols)

    def invert(l):
        main, rest, done = call(
            functools.partial(invert_body, l, lines),
            [vmem_out((levels, height, LANES)), vmem_out((height, LANES)), token],
            pivots,
            lower,
            upper,
            scratch=[
                pltpu.VMEM((levels, height, cols), f32),
                pltpu.VMEM(((levels + lines) * cols, LANES), f32),
                pltpu.VMEM(((levels + lines) * cols, LANES), f32),
            ],
            limit=32,
        )
        kept[l] = in_vmem(main), in_vmem(rest)
        return done

    return [functools.partial(invert, l) for l in range(lines)] + [pack], kept


def per_device(residual, recycle_basis, recycle_images, jacobian, neighbours, line_members,
               line_pivots, line_lower, line_upper):
    elems, cols = residual.shape
    doms, blks = lax.axis_size("dom"), lax.axis_size("blk")
    lines, levels = line_pivots.shape[:2]
    entries = float(elems * cols * doms * blks)
    count = float(elems * SAMPLE * doms * blks)
    dom, blk = lax.axis_index("dom"), lax.axis_index("blk")
    devices = doms * blks
    row = jax.ShapeDtypeStruct((1, LANES), f32)
    rows = jax.ShapeDtypeStruct((elems, cols), f32)

    members = line_members.reshape(devices, elems)
    near = jnp.array([(d, b) for d in range(-2, 3) for b in range(blks)], jnp.int32)
    at = (dom + near[:, 0] + doms) % doms * blks + (blk + near[:, 1]) % blks
    line_ids = members[at].reshape(-1)
    near_own = at[blks : 4 * blks]
    elem_ids = (near_own[:, None] * elems + jnp.arange(elems, dtype=jnp.int32)).reshape(-1)
    me = dom * blks + blk
    own_ids = me * elems + jnp.arange(elems, dtype=jnp.int32)
    wanted = jnp.concatenate([own_ids[None], neighbours.T], 0).reshape(-1)
    stencil = (wanted[:, None] == line_ids[None, :]).astype(f32)
    mine = lax.dynamic_slice_in_dim(members, me, 1, 0)[0]
    entering = (mine[:, None] == elem_ids[None, :]).astype(f32)
    stencil_pool = pltpu.VMEM((stencil.shape[1], cols), f32)

    sample_jac = jnp.transpose(jacobian[:, 0, :SAMPLE], (1, 0, 2))
    sample_pivots = jnp.transpose(line_pivots[:, :, :SAMPLE], (0, 2, 1, 3))
    part = call(project_body, row, recycle_images, residual, sample_jac, sample_pivots)
    calls, kept = matrices_of(jacobian, line_pivots, line_lower, line_upper)
    projected = added(part, calls)
    correction, start = call(
        functools.partial(deflate_body, entries),
        [rows, rows],
        projected,
        residual,
        recycle_basis,
        recycle_images,
    )

    def precondition(v, kept):
        z = call(
            functools.partial(solve_body, lines),
            rows,
            *around(v, 1),
            entering,
            *[kept[l][0] for l in range(lines)],
            *[kept[l][1] for l in range(lines)],
            scratch=[
                pltpu.VMEM((entering.shape[1], cols), f32),
                pltpu.VMEM((elems, ROWS, LANES), f32),
            ],
        )
        return around(z, 2)

    vectors = [start]
    matrix = jax.ShapeDtypeStruct((2 * STEPS, LANES), f32)
    for j in range(STEPS):
        last = j == STEPS - 1
        result = call(
            functools.partial(power_last_body if last else power_body, count),
            [rows, matrix] if last else rows,
            *precondition(vectors[-1], kept),
            *(vectors if last else ()),
            vectors[-1],
            projected,
            stencil,
            *kept["jac"],
            scratch=[stencil_pool],
        )
        vectors.append(result[0] if last else result)
    gram = added(result[1])
    small = jax.ShapeDtypeStruct((STEPS, LANES), f32)
    stacked = jax.ShapeDtypeStruct((STEPS + 1, elems, cols), f32)
    basis, hessenberg, norm, sure = call(
        functools.partial(combine_body, entries, count),
        [stacked, small, row, row],
        gram,
        projected,
        *vectors,
    )

    def stepwise(start):
        calls, kept = matrices_of(jacobian, line_pivots, line_lower, line_upper)
        for each in calls:
            each()
        matrices = (stencil, *kept["jac"])
        c, part = call(
            first_body,
            [rows, row],
            *precondition(start, kept),
            start,
            *matrices,
            scratch=[stencil_pool],
        )
        stack = jax.ShapeDtypeStruct((STEPS, elems, cols), f32)

        def step(_, state):
            basis, images, hessenberg, u, c, v, known, part = state
            return tuple(
                call(
                    functools.partial(next_body, entries),
                    [stack, stack, matrix, rows, rows, rows, row, row],
                    *precondition(v, kept),
                    *matrices,
                    added(part),
                    u,
                    c,
                    known,
                    basis,
                    images,
                    hessenberg,
                    scratch=[stencil_pool],
                )
            )

        empty = jnp.zeros(stack.shape, f32)
        known = jnp.zeros((1, LANES), f32).at[0, SCALE].set(1.0)
        state = (empty, empty, jnp.zeros(matrix.shape, f32), start, c, c, known, part)
        basis, _, hessenberg, u, c, _, known, part = lax.fori_loop(0, STEPS - 1, step, state)
        basis, hessenberg, u, known, part = call(
            functools.partial(last_body, entries),
            [stack, matrix, rows, row, row],
            added(part),
            u,
            c,
            known,
            basis,
            hessenberg,
        )
        return tuple(
            call(
                functools.partial(finish_body, entries),
                [stacked, small, row],
                added(part),
                u,
                known,
                basis,
                hessenberg,
            )
        )

    basis, hessenberg, norm = lax.cond(
        sure[0, 0] > 0.5, lambda start: (basis, hessenberg, norm), stepwise, start
    )
    return correction, basis, hessenberg[:, : STEPS + 1].T, norm[0, 0]


def solution(mesh):
    both = ("dom", "blk")
    in_specs = (
        P(both, None),
        P(None, both, None),
        P(None, both, None),
        P(both, None, None, None),
        P(both, None),
        P(),
        P(both, None, None, None),
        P(both, None, None, None),
        P(both, None, None, None),
    )
    out_specs = (P(both, None), P(None, both, None), P(), P())
    return jax.shard_map(
        per_device, mesh=mesh, in_specs=in_specs, out_specs=out_specs, check_vma=False
    )
```

```python
import functools

import jax
import jax.numpy as jnp
from jax import lax
from jax.experimental import pallas as pl
from jax.experimental.pallas import tpu as pltpu
from jax.sharding import PartitionSpec as P

STEPS = 8
EPS = 1e-06
KEPT = 2e-3
SAMPLE = 16
LANES = 128
ROWS = 136
INTERPRET = False
f32 = jnp.float32
bf16 = jnp.bfloat16
MIB = 1024 * 1024


def vmem_out(shape):
    if INTERPRET:
        return jax.ShapeDtypeStruct(shape, f32)
    return pltpu.VMEM(shape, f32)


def in_vmem(array):
    return array if INTERPRET else pltpu.with_memory_space_constraint(array, pltpu.VMEM)


def in_hbm(array):
    return array if INTERPRET else pltpu.with_memory_space_constraint(array, pltpu.HBM)


def call(body, out_shape, *args, scratch=(), limit=8, specs=None, after=None):
    spec = pl.BlockSpec(memory_space=pltpu.VMEM)
    specs = list(specs) if specs is not None else [spec] * len(args)
    inner, count = body, len(args)
    if after is not None:
        specs, args = specs + [pl.BlockSpec(memory_space=pl.ANY)], (*args, after)

        def body(*refs):
            inner(*refs[:count], *refs[count + 1 :])

    outs = out_shape if isinstance(out_shape, (list, tuple)) else None
    return pl.pallas_call(
        body,
        out_shape=out_shape,
        in_specs=specs,
        out_specs=[spec] * len(outs) if outs is not None else spec,
        scratch_shapes=list(scratch),
        compiler_params=pltpu.CompilerParams(vmem_limit_bytes=limit * MIB),
        interpret=INTERPRET,
    )(*args)


def pick(hits, pool):
    hits = hits.astype(bf16)
    high = pool.astype(bf16)
    rest = pool - high.astype(f32)
    mid = rest.astype(bf16)
    low = (rest - mid.astype(f32)).astype(bf16)
    dot = functools.partial(jnp.dot, preferred_element_type=f32)
    return dot(hits, high) + (dot(hits, mid) + dot(hits, low))


def halves(array):
    high = array.astype(bf16)
    return high, (array - high.astype(f32)).astype(bf16)


def product(left, right, dims):
    lh, ll = halves(left)
    rh, rl = halves(right)
    dot = lambda a, b: lax.dot_general(a, b, (dims, ((), ())), preferred_element_type=f32)
    return dot(lh, rh) + (dot(lh, rl) + dot(ll, rh))


def pack_body(jac_hbm, main_ref, rest_ref, token_ref):
    faces, rows, elems, cols = jac_hbm.shape
    chunk, group = 27, 9
    token_ref[...] = jnp.zeros(token_ref.shape, f32)
    extra = cols - LANES

    def step(block, at=None):
        at = (pl.program_id(0) if at is None else at) * chunk
        lane = lax.broadcasted_iota(jnp.int32, (elems, LANES), 1)

        def row(i):
            packed = jnp.zeros((elems, LANES), f32)
            for f in range(faces):
                main_ref[f, at + i] = block[f, i, :, 0:LANES]
                tail = jnp.concatenate(
                    [block[f, i, :, LANES:cols], jnp.zeros((elems, LANES - extra), f32)], 1
                )
                if f:
                    tail = pltpu.roll(tail, f * extra, 1)
                packed = packed + tail
            rest_ref[at + i] = packed

        def some(g, _):
            for n in range(group):
                row(g * group + n)
            return 0

        lax.fori_loop(0, chunk // group, some, 0)

    if INTERPRET:
        for c in range(rows // chunk):
            step(jac_hbm[:, c * chunk : (c + 1) * chunk], c)
        return
    pltpu.emit_pipeline(
        step,
        grid=(rows // chunk,),
        in_specs=[pl.BlockSpec((faces, chunk, elems, cols), lambda c: (0, c, 0, 0))],
    )(jac_hbm)


def invert_body(l, lines, pivot_ref, lower_ref, upper_ref, main_ref, rest_ref, token_ref, part_ref, wide_ref, side_ref):
    levels, height, _ = main_ref.shape
    cols = part_ref.shape[2]
    extra = cols - LANES
    rows_by_rows = ((1,), (1,))
    rows_by_cols = ((1,), (0,))
    pivot_rows = levels * cols
    token_ref[...] = jnp.zeros(token_ref.shape, f32)
    wide_ref[0:pivot_rows, :] = pivot_ref[l, :, 0:LANES]
    side_ref[0:pivot_rows, 0:extra] = pivot_ref[l, :, LANES:cols]

    def strided(first, count):
        at = pl.ds(first, cols, stride=count)
        return jnp.concatenate([wide_ref[at, :], side_ref[at, :][:, 0:extra]], 1)

    def paired(ref, k):
        wide_ref[pivot_rows:, :] = ref[k, :, 0:LANES]
        side_ref[pivot_rows:, 0:extra] = ref[k, :, LANES:cols]
        return strided(pivot_rows + l, lines)

    part_ref[...] = jnp.zeros(part_ref.shape, f32)
    part_ref[0, 0:cols, :] = strided(0, levels).T
    for k in range(1, levels):
        pivot = strided(k, levels)
        mixed = product(pivot, paired(lower_ref, k - 1), rows_by_cols)
        before = part_ref[k - 1, 0 : k * ROWS, :]
        part_ref[k, 0 : k * ROWS, :] = -product(before, mixed, rows_by_rows)
        part_ref[k, k * ROWS : k * ROWS + cols, :] = pivot.T

    def backward(i, _):
        k = levels - 2 - i
        part_ref[k] = part_ref[k] - product(part_ref[k + 1], paired(upper_ref, k), rows_by_rows)
        return 0

    lax.fori_loop(0, levels - 1, backward, 0)

    def emit(t, _):
        at = pl.ds(pl.multiple_of(t * ROWS, 8), ROWS)
        packed = jnp.zeros((ROWS, LANES), f32)
        for k in range(levels):
            main_ref[k, at, :] = part_ref[k, at, 0:LANES]
            tail = jnp.concatenate(
                [part_ref[k, at, LANES:cols], jnp.zeros((ROWS, LANES - extra), f32)], 1
            )
            packed = packed + (pltpu.roll(tail, k * extra, 1) if k else tail)
        rest_ref[at, :] = packed
        return 0

    lax.fori_loop(0, levels, emit, 0)


def solve_body(lines, copies, *refs):
    blocks, refs = refs[: -4 - 2 * lines], refs[-4 - 2 * lines :]
    hits_ref, out_ref, pool_ref, wide_ref = refs[0], *refs[-3:]
    mains, rests = refs[1 : 1 + lines], refs[1 + lines : 1 + 2 * lines]
    levels = mains[0].shape[0]
    count = hits_ref.shape[0]
    cols = pool_ref.shape[1]
    extra = cols - LANES
    fill_pool(blocks, pool_ref)
    rhs = pick(hits_ref[...], pool_ref[...])
    rhs = jnp.concatenate([rhs, jnp.zeros((count, 2 * LANES - cols), f32)], 1)
    rhs = rhs.T[0:ROWS]
    for q in range(count):
        wide_ref[q] = jnp.broadcast_to(rhs[:, q : q + 1], (ROWS, LANES))
    for l in range(lines):

        def member(m, sums):
            sums = list(sums)
            for t in range(ROWS // 8):
                at = pl.ds(pl.multiple_of(m * ROWS + t * 8, 8), 8)
                value = wide_ref[l * levels + m, t * 8 : t * 8 + 8, :]
                for k in range(levels):
                    sums[k] = sums[k] + mains[l][k, at, :] * value
                sums[levels] = sums[levels] + rests[l][at, :] * value
            return tuple(sums)

        zero = jnp.zeros((8, LANES), f32)
        sums = lax.fori_loop(0, levels, member, (zero,) * (levels + 1))
        tails = jnp.sum(sums[levels], axis=0, keepdims=True)
        tails = jnp.broadcast_to(tails, (8, LANES))
        for k in range(levels):
            total = jnp.sum(sums[k], axis=0, keepdims=True)
            tail = pltpu.roll(tails, LANES - k * extra, 1) if k else tails
            for n in range(copies):
                at = slice(n * count + l * levels + k, n * count + l * levels + k + 1)
                out_ref[at, 0:LANES] = total
                out_ref[at, LANES:cols] = tail[0:1, 0:extra]


def fill_pool(blocks, pool_ref):
    at = 0
    for block in blocks:
        count = block.shape[0]
        pool_ref[at : at + count, :] = block[...]
        at += count


def operate(blocks, hits_ref, main_ref, rest_ref, pool_ref):
    faces, rows, elems, _ = main_ref.shape
    cols = pool_ref.shape[1]
    extra = cols - LANES
    fill_pool(blocks, pool_ref)
    field = pick(hits_ref[...], pool_ref[...])
    heads = [field[f * elems : (f + 1) * elems, 0:LANES] for f in range(faces)]
    packed = jnp.zeros((elems, LANES), f32)
    for f in range(faces):
        tail = jnp.concatenate(
            [field[f * elems : (f + 1) * elems, LANES:cols], jnp.zeros((elems, LANES - extra), f32)], 1
        )
        packed = packed + (pltpu.roll(tail, f * extra, 1) if f else tail)
    lane = lax.broadcasted_iota(jnp.int32, (elems, LANES), 1)

    def one(i):
        total = rest_ref[i] * packed
        for f in range(faces):
            total = total + main_ref[f, i] * heads[f]
        return jnp.sum(total, axis=1, keepdims=True)

    group = 16

    def some(g, image):
        for s in range(group):
            i = g * group + s
            image = jnp.where(lane == i, one(i), image)
        return image

    image = lax.fori_loop(0, LANES // group, some, jnp.zeros((elems, LANES), f32))
    tail = jnp.zeros((elems, LANES), f32)
    for c in range(extra):
        tail = jnp.where(lane == c, one(LANES + c), tail)
    return jnp.concatenate([image, tail[:, 0:extra]], 1)


def row_of(values):
    lane = lax.broadcasted_iota(jnp.int32, (1, LANES), 1)
    row = jnp.zeros((1, LANES), f32)
    for i, value in values.items():
        total = jnp.sum(jnp.sum(value, axis=0, keepdims=True), axis=1, keepdims=True)
        row = jnp.where(lane == i, total, row)
    return row


def lane_of(row, i):
    return row[:, i : i + 1]


UC, UU, CC = 13, 14, 15
SHIFT, SCALE, STEP = 0, 1, 2


def totals(parts_ref):
    return jnp.sum(parts_ref[...], axis=0, keepdims=True)


def project_body(images_ref, residual_ref, jac_ref, pivot_ref, out_ref):
    residual = residual_ref[...]
    products = {k: images_ref[k] * residual for k in range(STEPS)}
    lane = lax.broadcasted_iota(jnp.int32, jac_ref.shape[1:], 1)
    own = jnp.zeros(jac_ref.shape[1:], f32)
    for i in range(SAMPLE):
        own = jnp.where(lane == i, jac_ref[i], own)
    products[STEPS] = own
    lines, _, levels, _ = pivot_ref.shape
    lane = lax.broadcasted_iota(jnp.int32, pivot_ref.shape[2:], 1)
    own = jnp.zeros(pivot_ref.shape[2:], f32)
    for l in range(lines):
        for i in range(SAMPLE):
            own = own + jnp.where(lane == i, pivot_ref[l, i], 0.0)
    products[STEPS + 1] = own
    out_ref[...] = row_of(products)


def deflate_body(entries, parts_ref, residual_ref, basis_ref, images_ref, correction_ref, start_ref):
    row = totals(parts_ref) / entries
    correction = jnp.zeros(residual_ref.shape, f32)
    start = residual_ref[...]
    for k in range(basis_ref.shape[0]):
        weight = lane_of(row, k)
        correction = correction + weight * basis_ref[k]
        start = start - weight * images_ref[k]
    correction_ref[...] = correction
    start_ref[...] = start


def shift_of(row, count):
    return lane_of(row, STEPS) / count * (lane_of(row, STEPS + 1) / count)


def power_body(count, *refs):
    *blocks, u_ref, row_ref, hits_ref, main_ref, rest_ref, out_ref, pool_ref = refs
    image = operate(blocks, hits_ref, main_ref, rest_ref, pool_ref)
    out_ref[...] = image - shift_of(row_ref[...], count) * u_ref[...]


def power_last_body(count, *refs):
    blocks, vectors, refs = refs[: -8 - STEPS], refs[-8 - STEPS : -8], refs[-8:]
    u_ref, row_ref, hits_ref, main_ref, rest_ref, out_ref, part_ref, pool_ref = refs
    image = operate(blocks, hits_ref, main_ref, rest_ref, pool_ref)
    last = image - shift_of(row_ref[...], count) * u_ref[...]
    out_ref[...] = last
    vectors = [v[...] for v in vectors] + [last]
    at = lax.broadcasted_iota(jnp.int32, part_ref.shape, 0)
    lane = lax.broadcasted_iota(jnp.int32, part_ref.shape, 1)
    part = jnp.zeros(part_ref.shape, f32)
    for k, right in enumerate(vectors):
        for i in range(k + 1):
            total = jnp.sum(vectors[i] * right, axis=0, keepdims=True)
            total = jnp.sum(total, axis=1, keepdims=True)
            here = ((at == i) & (lane == k)) | ((at == k) & (lane == i))
            part = jnp.where(here, total, part)
    part_ref[...] = part


def combine_body(entries, count, *refs):
    gram_ref, row_ref, *vectors = refs[: 3 + STEPS]
    basis_out, hess_out, norm_ref, sure_ref = refs[3 + STEPS :]
    shift = shift_of(row_ref[...], count)
    gram = gram_ref[...] / entries
    size = jnp.abs(gram)
    at = lax.broadcasted_iota(jnp.int32, gram.shape, 0)
    lane = lax.broadcasted_iota(jnp.int32, gram.shape, 1)

    def across(values):
        return jnp.sum(values, axis=1, keepdims=True)

    def turned(column):
        return jnp.sum(jnp.where(at == lane, column, 0.0), axis=0, keepdims=True)

    def times(matrix, row):
        return turned(across(matrix * row))

    first = lane[0:1]
    norm = jnp.sqrt(gram[0:1, 0:1] + EPS)
    norm_ref[...] = jnp.broadcast_to(norm, (1, LANES))
    newest = jnp.where(first == 0, 1.0 / norm, 0.0)
    known = jnp.where(at == 0, newest, 0.0)
    sure = jnp.full((1, 1), 1.0, f32)
    for j in range(STEPS):
        moved = pltpu.roll(jnp.broadcast_to(newest, (8, LANES)), 1, 1)[0:1]
        image = moved + shift * newest
        inner = across(known * times(gram, image))
        reduced = image - jnp.sum(known * inner, axis=0, keepdims=True)
        square = across(reduced * times(gram, reduced))
        terms = across(jnp.abs(reduced) * times(size, jnp.abs(reduced)))
        sure = jnp.where(square > KEPT * terms, sure, 0.0)
        below = jnp.sqrt(jnp.maximum(square, 0.0) + EPS)
        column = jnp.where(first <= j, turned(inner), 0.0)
        hess_out[j : j + 1, :] = jnp.where(first == j + 1, below, column)
        newest = reduced / below
        known = jnp.where(at == j + 1, newest, known)
    sure_ref[...] = jnp.broadcast_to(sure, (1, LANES))
    vectors = [v[...] for v in vectors]
    for j in range(STEPS + 1):
        value = known[j : j + 1, 0:1] * vectors[0]
        for k in range(1, j + 1):
            value = value + known[j : j + 1, k : k + 1] * vectors[k]
        basis_out[j] = value


def first_body(*refs):
    *blocks, u_ref, hits_ref, main_ref, rest_ref, c_ref, part_ref, pool_ref = refs
    c = operate(blocks, hits_ref, main_ref, rest_ref, pool_ref)
    c_ref[...] = c
    u = u_ref[...]
    part_ref[...] = row_of({UC: u * c, UU: u * u, CC: c * c})


def advance(entries, row, u, c, known, basis):
    scale, step = lane_of(known, SCALE), lane_of(known, STEP)
    norm = jnp.sqrt(lane_of(row, UU) / entries + EPS / (scale * scale))
    inverse = 1.0 / norm
    here = u * inverse
    image = c * inverse
    lane = lax.broadcasted_iota(jnp.int32, (1, LANES), 1)
    own = lane_of(row, UC) * inverse * inverse / entries
    column = jnp.where(lane < STEPS, row * inverse / entries, 0.0)
    column = jnp.where(lane.astype(f32) == step, own, column)
    scale_next = jnp.sqrt(lane_of(row, CC) * inverse * inverse / entries + EPS)
    reduced = image - own * here
    for i in range(STEPS):
        reduced = reduced - lane_of(row, i) * inverse / entries * basis[i]
    return here, image, inverse, own, column, scale * norm, reduced / scale_next, scale_next


def place(out_ref, in_ref, step, value):
    for i in range(in_ref.shape[0]):
        out_ref[i] = jnp.where(step == i, value, in_ref[i])


def record(hess_out, hess_ref, step, column, below):
    at = lax.broadcasted_iota(jnp.int32, hess_ref.shape, 0).astype(f32)
    lane = lax.broadcasted_iota(jnp.int32, hess_ref.shape, 1).astype(f32)
    hess = jnp.where(at == step, column, hess_ref[...])
    hess_out[...] = jnp.where((at == STEPS) & (lane == step), below, hess)


def numbers(shift, scale, step):
    lane = lax.broadcasted_iota(jnp.int32, (1, LANES), 1)
    row = jnp.where(lane == SHIFT, shift, jnp.zeros((1, LANES), f32))
    row = jnp.where(lane == SCALE, scale, row)
    return jnp.where(lane == STEP, step, row)


def next_body(entries, *refs):
    *blocks, hits_ref, main_ref, rest_ref, sums_ref, u_ref, c_ref, known_ref = refs[:-12]
    basis_ref, images_ref, hess_ref, basis_out, images_out, hess_out = refs[-12:-6]
    u_out, c_out, v_out, known_out, part_ref, pool_ref = refs[-6:]
    w = operate(blocks, hits_ref, main_ref, rest_ref, pool_ref)
    known = known_ref[...]
    step = lane_of(known, STEP)
    row = totals(sums_ref)
    here, image, inverse, own, column, below, u, scale = advance(
        entries, row, u_ref[...], c_ref[...], known, basis_ref
    )
    moved = w * inverse - (own - lane_of(known, SHIFT)) * image
    for i in range(STEPS):
        moved = moved - lane_of(row, i) * inverse / entries * images_ref[i]
    c = moved / scale
    place(basis_out, basis_ref, step, here)
    place(images_out, images_ref, step, image)
    record(hess_out, hess_ref, step, column, below)
    u_out[...] = u
    c_out[...] = c
    v_out[...] = c - own * u
    known_out[...] = numbers(own, scale, step + 1.0)
    products = {i: jnp.where(step == i, here, basis_ref[i]) * c for i in range(STEPS)}
    products.update({UC: u * c, UU: u * u, CC: c * c})
    part_ref[...] = row_of(products)


def last_body(entries, sums_ref, u_ref, c_ref, known_ref, basis_ref, hess_ref, *outs):
    basis_out, hess_out, u_out, known_out, part_ref = outs
    known = known_ref[...]
    step = lane_of(known, STEP)
    here, _, _, own, column, below, u, scale = advance(
        entries, totals(sums_ref), u_ref[...], c_ref[...], known, basis_ref
    )
    place(basis_out, basis_ref, step, here)
    record(hess_out, hess_ref, step, column, below)
    u_out[...] = u
    known_out[...] = numbers(own, scale, step + 1.0)
    part_ref[...] = row_of({UU: u * u})


def finish_body(entries, sums_ref, u_ref, known_ref, basis_ref, hess_ref, basis_out, hess_out, norm_ref):
    scale = lane_of(known_ref[...], SCALE)
    norm = jnp.sqrt(lane_of(totals(sums_ref), UU) / entries + EPS / (scale * scale))
    for i in range(STEPS):
        basis_out[i] = basis_ref[i]
    basis_out[STEPS] = u_ref[...] / norm
    lane = lax.broadcasted_iota(jnp.int32, (1, LANES), 1)
    norms = hess_ref[STEPS : STEPS + 1, :]
    for j in range(STEPS):
        below = lane_of(norms, j + 1) if j + 1 < STEPS else scale * norm
        hess_out[j : j + 1, :] = jnp.where(lane == j + 1, below, hess_ref[j : j + 1, :])
    norm_ref[...] = norms


def shifted(array, d_dom, d_blk):
    doms, blks = lax.axis_size("dom"), lax.axis_size("blk")
    if d_dom == 0 and d_blk == 0:
        return array
    pairs = []
    for d in range(doms):
        for b in range(blks):
            source = ((d + d_dom) % doms) * blks + (b + d_blk) % blks
            pairs.append((source, d * blks + b))
    return lax.ppermute(array, ("dom", "blk"), pairs)


def around(array, reach):
    blks = lax.axis_size("blk")
    whole = jnp.concatenate([shifted(array, 0, b) for b in range(blks)], 0)
    return [shifted(whole, d, 0) for d in range(-reach, reach + 1)]


def added(part, beside=()):
    beside = list(beside)
    doms, blks = lax.axis_size("dom"), lax.axis_size("blk")
    devices = doms * blks
    reach = 1
    while reach < devices:
        ways = 4 if reach * 4 <= devices else 2
        others = [
            lax.ppermute(part, ("dom", "blk"), [(n ^ (k * reach), n) for n in range(devices)])
            for k in range(1, ways)
        ]
        if ways == 4:
            part = (part + others[0]) + (others[1] + others[2])
        else:
            part = part + others[0]
        work = beside.pop(0) if beside else None
        if work is not None:
            part = part + work()
        reach *= ways
    return part


def matrices_of(jacobian, line_pivots, line_lower, line_upper):
    elems, faces, cols, _ = jacobian.shape
    lines, levels = line_pivots.shape[:2]
    height = levels * ROWS
    token = jax.ShapeDtypeStruct((1, LANES), f32)
    kept = {}

    def pack(after=None):
        main, rest, done = call(
            pack_body,
            [vmem_out((faces, cols, elems, LANES)), vmem_out((cols, elems, LANES)), token],
            in_hbm(jnp.transpose(jacobian, (1, 2, 0, 3))),
            specs=[pl.BlockSpec(memory_space=pltpu.VMEM if INTERPRET else pltpu.HBM)],
            limit=8,
            after=after,
        )
        kept["jac"] = in_vmem(main), in_vmem(rest)
        return done

    pivots = jnp.transpose(line_pivots, (0, 2, 1, 3)).reshape(lines, cols * levels, cols)
    lower = jnp.transpose(line_lower, (1, 2, 0, 3)).reshape(levels - 1, cols * lines, cols)
    upper = jnp.transpose(line_upper, (1, 2, 0, 3)).reshape(levels - 1, cols * lines, cols)

    def invert(l, after=None):
        main, rest, done = call(
            functools.partial(invert_body, l, lines),
            [vmem_out((levels, height, LANES)), vmem_out((height, LANES)), token],
            pivots,
            lower,
            upper,
            scratch=[
                pltpu.VMEM((levels, height, cols), f32),
                pltpu.VMEM(((levels + lines) * cols, LANES), f32),
                pltpu.VMEM(((levels + lines) * cols, LANES), f32),
            ],
            limit=20,
            after=after,
        )
        kept[l] = in_vmem(main), in_vmem(rest)
        return done

    return invert, pack, kept


def per_device(residual, recycle_basis, recycle_images, jacobian, neighbours, line_members,
               line_pivots, line_lower, line_upper):
    elems, cols = residual.shape
    doms, blks = lax.axis_size("dom"), lax.axis_size("blk")
    lines, levels = line_pivots.shape[:2]
    entries = float(elems * cols * doms * blks)
    count = float(elems * SAMPLE * doms * blks)
    dom, blk = lax.axis_index("dom"), lax.axis_index("blk")
    devices = doms * blks
    row = jax.ShapeDtypeStruct((1, LANES), f32)
    rows = jax.ShapeDtypeStruct((elems, cols), f32)

    members = line_members.reshape(devices, elems)
    near = jnp.array([(d, b) for d in range(-2, 3) for b in range(blks)], jnp.int32)
    first = (dom + near[:, 0] + doms) % doms * blks
    line_ids = members[first + near[:, 1]].reshape(-1)
    near_own = (first + (blk + near[:, 1]) % blks)[blks : 4 * blks]
    elem_ids = (near_own[:, None] * elems + jnp.arange(elems, dtype=jnp.int32)).reshape(-1)
    me = dom * blks + blk
    own_ids = me * elems + jnp.arange(elems, dtype=jnp.int32)
    wanted = jnp.concatenate([own_ids[None], neighbours.T], 0).reshape(-1)
    stencil = (wanted[:, None] == line_ids[None, :]).astype(f32)
    mine = lax.dynamic_slice_in_dim(members, me, 1, 0)[0]
    entering = (mine[:, None] == elem_ids[None, :]).astype(f32)
    stencil_pool = pltpu.VMEM((stencil.shape[1], cols), f32)

    sample_jac = jnp.transpose(jacobian[:, 0, :SAMPLE], (1, 0, 2))
    sample_pivots = jnp.transpose(line_pivots[:, :, :SAMPLE], (0, 2, 1, 3))
    part = call(project_body, row, recycle_images, residual, sample_jac, sample_pivots)
    invert, pack, kept = matrices_of(jacobian, line_pivots, line_lower, line_upper)
    projected = added(part, [None, functools.partial(invert, 0)])
    correction, start = call(
        functools.partial(deflate_body, entries),
        [rows, rows],
        projected,
        residual,
        recycle_basis,
        recycle_images,
    )

    for l in range(1, lines):
        invert(l, start)

    def precondition(v, kept, then=None):
        copies = call(
            functools.partial(solve_body, lines, blks),
            jax.ShapeDtypeStruct((blks * elems, cols), f32),
            *around(v, 1),
            entering,
            *[kept[l][0] for l in range(lines)],
            *[kept[l][1] for l in range(lines)],
            scratch=[
                pltpu.VMEM((entering.shape[1], cols), f32),
                pltpu.VMEM((elems, ROWS, LANES), f32),
            ],
        )
        if then is not None:
            then(copies)
        whole = lax.all_to_all(copies, "blk", 0, 0, tiled=True)
        return [shifted(whole, d, 0) for d in range(-2, 3)]

    vectors = [start]
    matrix = jax.ShapeDtypeStruct((2 * STEPS, LANES), f32)
    for j in range(STEPS):
        last = j == STEPS - 1
        pool = precondition(vectors[-1], kept, pack if j == 0 else None)
        result = call(
            functools.partial(power_last_body if last else power_body, count),
            [rows, matrix] if last else rows,
            *pool,
            *(vectors if last else ()),
            vectors[-1],
            projected,
            stencil,
            *kept["jac"],
            scratch=[stencil_pool],
        )
        vectors.append(result[0] if last else result)
    gram = added(result[1])
    small = jax.ShapeDtypeStruct((STEPS, LANES), f32)
    stacked = jax.ShapeDtypeStruct((STEPS + 1, elems, cols), f32)
    basis, hessenberg, norm, sure = call(
        functools.partial(combine_body, entries, count),
        [stacked, small, row, row],
        gram,
        projected,
        *vectors,
    )

    def stepwise(start):
        invert, pack, kept = matrices_of(jacobian, line_pivots, line_lower, line_upper)
        for l in range(lines):
            invert(l)
        pack()
        matrices = (stencil, *kept["jac"])
        c, part = call(
            first_body,
            [rows, row],
            *precondition(start, kept),
            start,
            *matrices,
            scratch=[stencil_pool],
        )
        stack = jax.ShapeDtypeStruct((STEPS, elems, cols), f32)

        def step(_, state):
            basis, images, hessenberg, u, c, v, known, part = state
            return tuple(
                call(
                    functools.partial(next_body, entries),
                    [stack, stack, matrix, rows, rows, rows, row, row],
                    *precondition(v, kept),
                    *matrices,
                    added(part),
                    u,
                    c,
                    known,
                    basis,
                    images,
                    hessenberg,
                    scratch=[stencil_pool],
                )
            )

        empty = jnp.zeros(stack.shape, f32)
        known = jnp.zeros((1, LANES), f32).at[0, SCALE].set(1.0)
        state = (empty, empty, jnp.zeros(matrix.shape, f32), start, c, c, known, part)
        basis, _, hessenberg, u, c, _, known, part = lax.fori_loop(0, STEPS - 1, step, state)
        basis, hessenberg, u, known, part = call(
            functools.partial(last_body, entries),
            [stack, matrix, rows, row, row],
            added(part),
            u,
            c,
            known,
            basis,
            hessenberg,
        )
        return tuple(
            call(
                functools.partial(finish_body, entries),
                [stacked, small, row],
                added(part),
                u,
                known,
                basis,
                hessenberg,
            )
        )

    basis, hessenberg, norm = lax.cond(
        sure[0, 0] > 0.5, lambda start: (basis, hessenberg, norm), stepwise, start
    )
    return correction, basis, hessenberg[:, : STEPS + 1].T, norm[0, 0]


def solution(mesh):
    both = ("dom", "blk")
    in_specs = (
        P(both, None),
        P(None, both, None),
        P(None, both, None),
        P(both, None, None, None),
        P(both, None),
        P(),
        P(both, None, None, None),
        P(both, None, None, None),
        P(both, None, None, None),
    )
    out_specs = (P(both, None), P(None, both, None), P(), P())
    return jax.shard_map(
        per_device, mesh=mesh, in_specs=in_specs, out_specs=out_specs, check_vma=False
    )
```

```python
import functools

import jax
import jax.numpy as jnp
from jax import lax
from jax.experimental import pallas as pl
from jax.experimental.pallas import tpu as pltpu
from jax.sharding import PartitionSpec as P

STEPS = 8
EPS = 1e-06
KEPT = 2e-3
SAMPLE = 16
LANES = 128
ROWS = 136
INTERPRET = False
f32 = jnp.float32
bf16 = jnp.bfloat16
MIB = 1024 * 1024


def vmem_out(shape):
    if INTERPRET:
        return jax.ShapeDtypeStruct(shape, f32)
    return pltpu.VMEM(shape, f32)


def in_vmem(array):
    return array if INTERPRET else pltpu.with_memory_space_constraint(array, pltpu.VMEM)


def in_hbm(array):
    return array if INTERPRET else pltpu.with_memory_space_constraint(array, pltpu.HBM)


def call(body, out_shape, *args, scratch=(), limit=8, specs=None, after=None):
    spec = pl.BlockSpec(memory_space=pltpu.VMEM)
    specs = list(specs) if specs is not None else [spec] * len(args)
    inner, count = body, len(args)
    if after is not None:
        specs, args = specs + [pl.BlockSpec(memory_space=pl.ANY)], (*args, after)

        def body(*refs):
            inner(*refs[:count], *refs[count + 1 :])

    outs = out_shape if isinstance(out_shape, (list, tuple)) else None
    return pl.pallas_call(
        body,
        out_shape=out_shape,
        in_specs=specs,
        out_specs=[spec] * len(outs) if outs is not None else spec,
        scratch_shapes=list(scratch),
        compiler_params=pltpu.CompilerParams(vmem_limit_bytes=limit * MIB),
        interpret=INTERPRET,
    )(*args)


def pick(hits, pool):
    hits = hits.astype(bf16)
    high = pool.astype(bf16)
    rest = pool - high.astype(f32)
    mid = rest.astype(bf16)
    low = (rest - mid.astype(f32)).astype(bf16)
    dot = functools.partial(jnp.dot, preferred_element_type=f32)
    return dot(hits, high) + (dot(hits, mid) + dot(hits, low))


def halves(array):
    high = array.astype(bf16)
    return high, (array - high.astype(f32)).astype(bf16)


def product(left, right, dims):
    lh, ll = halves(left)
    rh, rl = halves(right)
    dot = lambda a, b: lax.dot_general(a, b, (dims, ((), ())), preferred_element_type=f32)
    return dot(lh, rh) + (dot(lh, rl) + dot(ll, rh))


def zero_body(*refs):
    refs[-1][...] = jnp.zeros(refs[-1].shape, f32)


def pack_body(jac_hbm, main_ref, rest_ref, token_ref):
    faces, rows, elems, cols = jac_hbm.shape
    chunk, group = 27, 9
    token_ref[...] = jnp.zeros(token_ref.shape, f32)
    extra = cols - LANES

    def step(block, at=None):
        at = (pl.program_id(0) if at is None else at) * chunk
        lane = lax.broadcasted_iota(jnp.int32, (elems, LANES), 1)

        def row(i):
            packed = jnp.zeros((elems, LANES), f32)
            for f in range(faces):
                main_ref[f, at + i] = block[f, i, :, 0:LANES]
                tail = jnp.concatenate(
                    [block[f, i, :, LANES:cols], jnp.zeros((elems, LANES - extra), f32)], 1
                )
                if f:
                    tail = pltpu.roll(tail, f * extra, 1)
                packed = packed + tail
            rest_ref[at + i] = packed

        def some(g, _):
            for n in range(group):
                row(g * group + n)
            return 0

        lax.fori_loop(0, chunk // group, some, 0)

    if INTERPRET:
        for c in range(rows // chunk):
            step(jac_hbm[:, c * chunk : (c + 1) * chunk], c)
        return
    pltpu.emit_pipeline(
        step,
        grid=(rows // chunk,),
        in_specs=[pl.BlockSpec((faces, chunk, elems, cols), lambda c: (0, c, 0, 0))],
    )(jac_hbm)


def invert_body(l, lines, pivot_ref, lower_ref, upper_ref, main_ref, rest_ref, token_ref, part_ref, wide_ref, side_ref):
    levels, height, _ = main_ref.shape
    cols = part_ref.shape[2]
    extra = cols - LANES
    rows_by_rows = ((1,), (1,))
    rows_by_cols = ((1,), (0,))
    pivot_rows = levels * cols
    token_ref[...] = jnp.zeros(token_ref.shape, f32)
    wide_ref[0:pivot_rows, :] = pivot_ref[l, :, 0:LANES]
    side_ref[0:pivot_rows, 0:extra] = pivot_ref[l, :, LANES:cols]

    def strided(first, count):
        at = pl.ds(first, cols, stride=count)
        return jnp.concatenate([wide_ref[at, :], side_ref[at, :][:, 0:extra]], 1)

    def paired(ref, k):
        wide_ref[pivot_rows:, :] = ref[k, :, 0:LANES]
        side_ref[pivot_rows:, 0:extra] = ref[k, :, LANES:cols]
        return strided(pivot_rows + l, lines)

    part_ref[...] = jnp.zeros(part_ref.shape, f32)
    part_ref[0, 0:cols, :] = strided(0, levels).T
    for k in range(1, levels):
        pivot = strided(k, levels)
        mixed = product(pivot, paired(lower_ref, k - 1), rows_by_cols)
        before = part_ref[k - 1, 0 : k * ROWS, :]
        part_ref[k, 0 : k * ROWS, :] = -product(before, mixed, rows_by_rows)
        part_ref[k, k * ROWS : k * ROWS + cols, :] = pivot.T

    def backward(i, _):
        k = levels - 2 - i
        part_ref[k] = part_ref[k] - product(part_ref[k + 1], paired(upper_ref, k), rows_by_rows)
        return 0

    lax.fori_loop(0, levels - 1, backward, 0)

    def emit(t, _):
        at = pl.ds(pl.multiple_of(t * ROWS, 8), ROWS)
        packed = jnp.zeros((ROWS, LANES), f32)
        for k in range(levels):
            main_ref[k, at, :] = part_ref[k, at, 0:LANES]
            tail = jnp.concatenate(
                [part_ref[k, at, LANES:cols], jnp.zeros((ROWS, LANES - extra), f32)], 1
            )
            packed = packed + (pltpu.roll(tail, k * extra, 1) if k else tail)
        rest_ref[at, :] = packed
        return 0

    lax.fori_loop(0, levels, emit, 0)


def solve_body(lines, *refs):
    blocks, refs = refs[: -4 - 2 * lines], refs[-4 - 2 * lines :]
    hits_ref, out_ref, pool_ref, wide_ref = refs[0], *refs[-3:]
    mains, rests = refs[1 : 1 + lines], refs[1 + lines : 1 + 2 * lines]
    levels = mains[0].shape[0]
    count = hits_ref.shape[0]
    cols = pool_ref.shape[1]
    extra = cols - LANES
    fill_pool(blocks, pool_ref)
    rhs = pick(hits_ref[...], pool_ref[...])
    rhs = jnp.concatenate([rhs, jnp.zeros((count, 2 * LANES - cols), f32)], 1)
    rhs = rhs.T[0:ROWS]
    for q in range(count):
        wide_ref[q] = jnp.broadcast_to(rhs[:, q : q + 1], (ROWS, LANES))
    for l in range(lines):

        def member(m, sums):
            sums = list(sums)
            for t in range(ROWS // 8):
                at = pl.ds(pl.multiple_of(m * ROWS + t * 8, 8), 8)
                value = wide_ref[l * levels + m, t * 8 : t * 8 + 8, :]
                for k in range(levels):
                    sums[k] = sums[k] + mains[l][k, at, :] * value
                sums[levels] = sums[levels] + rests[l][at, :] * value
            return tuple(sums)

        zero = jnp.zeros((8, LANES), f32)
        sums = lax.fori_loop(0, levels, member, (zero,) * (levels + 1))
        tails = jnp.sum(sums[levels], axis=0, keepdims=True)
        tails = jnp.broadcast_to(tails, (8, LANES))
        for k in range(levels):
            total = jnp.sum(sums[k], axis=0, keepdims=True)
            tail = pltpu.roll(tails, LANES - k * extra, 1) if k else tails
            at = slice(l * levels + k, l * levels + k + 1)
            out_ref[at, 0:LANES] = total
            out_ref[at, LANES:cols] = tail[0:1, 0:extra]


def fill_pool(blocks, pool_ref):
    at = 0
    for block in blocks:
        count = block.shape[0]
        pool_ref[at : at + count, :] = block[...]
        at += count


def operate(blocks, hits_ref, main_ref, rest_ref, pool_ref):
    faces, rows, elems, _ = main_ref.shape
    cols = pool_ref.shape[1]
    extra = cols - LANES
    fill_pool(blocks, pool_ref)
    field = pick(hits_ref[...], pool_ref[...])
    heads = [field[f * elems : (f + 1) * elems, 0:LANES] for f in range(faces)]
    packed = jnp.zeros((elems, LANES), f32)
    for f in range(faces):
        tail = jnp.concatenate(
            [field[f * elems : (f + 1) * elems, LANES:cols], jnp.zeros((elems, LANES - extra), f32)], 1
        )
        packed = packed + (pltpu.roll(tail, f * extra, 1) if f else tail)
    lane = lax.broadcasted_iota(jnp.int32, (elems, LANES), 1)

    def one(i):
        total = rest_ref[i] * packed
        for f in range(faces):
            total = total + main_ref[f, i] * heads[f]
        return jnp.sum(total, axis=1, keepdims=True)

    group = 16

    def some(g, image):
        for s in range(group):
            i = g * group + s
            image = jnp.where(lane == i, one(i), image)
        return image

    image = lax.fori_loop(0, LANES // group, some, jnp.zeros((elems, LANES), f32))
    tail = jnp.zeros((elems, LANES), f32)
    for c in range(extra):
        tail = jnp.where(lane == c, one(LANES + c), tail)
    return jnp.concatenate([image, tail[:, 0:extra]], 1)


def row_of(values):
    lane = lax.broadcasted_iota(jnp.int32, (1, LANES), 1)
    row = jnp.zeros((1, LANES), f32)
    for i, value in values.items():
        total = jnp.sum(jnp.sum(value, axis=0, keepdims=True), axis=1, keepdims=True)
        row = jnp.where(lane == i, total, row)
    return row


def lane_of(row, i):
    return row[:, i : i + 1]


UC, UU, CC = 13, 14, 15
SHIFT, SCALE, STEP = 0, 1, 2


def totals(parts_ref):
    return jnp.sum(parts_ref[...], axis=0, keepdims=True)


def project_body(images_in, residual_in, jac_in, pivot_in, out_ref, *refs):
    lines, levels = pivot_in.shape[0], pivot_in.shape[1] // jac_in.shape[1]
    sources = [
        images_in,
        residual_in,
        jac_in.at[0, 0:SAMPLE],
        pivot_in.at[:, 0 : SAMPLE * levels, :],
    ]
    if INTERPRET:
        refs = [source[...] for source in sources]
    else:
        *refs, sems = refs
        copies = [
            pltpu.make_async_copy(source, ref, sems.at[n])
            for n, (source, ref) in enumerate(zip(sources, refs))
        ]
        for copy in copies:
            copy.start()
        for copy in copies:
            copy.wait()
    images_ref, residual_ref, jac_ref, pivot_ref = refs
    residual = residual_ref[...]
    products = {k: images_ref[k] * residual for k in range(STEPS)}
    lane = lax.broadcasted_iota(jnp.int32, jac_ref.shape[1:], 1)
    own = jnp.zeros(jac_ref.shape[1:], f32)
    for i in range(SAMPLE):
        own = jnp.where(lane == i, jac_ref[i], own)
    products[STEPS] = own
    shape = (levels, pivot_ref.shape[2])
    lane = lax.broadcasted_iota(jnp.int32, shape, 1)
    own = jnp.zeros(shape, f32)
    for l in range(lines):
        for i in range(SAMPLE):
            own = own + jnp.where(lane == i, pivot_ref[l, i * levels : (i + 1) * levels], 0.0)
    products[STEPS + 1] = own
    out_ref[...] = row_of(products)


def deflate_body(entries, parts_ref, residual_ref, basis_ref, images_ref, correction_ref, start_ref):
    row = totals(parts_ref) / entries
    correction = jnp.zeros(residual_ref.shape, f32)
    start = residual_ref[...]
    for k in range(basis_ref.shape[0]):
        weight = lane_of(row, k)
        correction = correction + weight * basis_ref[k]
        start = start - weight * images_ref[k]
    correction_ref[...] = correction
    start_ref[...] = start


def shift_of(row, count):
    return lane_of(row, STEPS) / count * (lane_of(row, STEPS + 1) / count)


def power_body(count, *refs):
    *blocks, u_ref, row_ref, hits_ref, main_ref, rest_ref, out_ref, pool_ref = refs
    image = operate(blocks, hits_ref, main_ref, rest_ref, pool_ref)
    out_ref[...] = image - shift_of(row_ref[...], count) * u_ref[...]


def power_last_body(count, *refs):
    blocks, vectors, refs = refs[: -8 - STEPS], refs[-8 - STEPS : -8], refs[-8:]
    u_ref, row_ref, hits_ref, main_ref, rest_ref, out_ref, part_ref, pool_ref = refs
    image = operate(blocks, hits_ref, main_ref, rest_ref, pool_ref)
    last = image - shift_of(row_ref[...], count) * u_ref[...]
    out_ref[...] = last
    vectors = [v[...] for v in vectors] + [last]
    at = lax.broadcasted_iota(jnp.int32, part_ref.shape, 0)
    lane = lax.broadcasted_iota(jnp.int32, part_ref.shape, 1)
    part = jnp.zeros(part_ref.shape, f32)
    for k, right in enumerate(vectors):
        for i in range(k + 1):
            total = jnp.sum(vectors[i] * right, axis=0, keepdims=True)
            total = jnp.sum(total, axis=1, keepdims=True)
            here = ((at == i) & (lane == k)) | ((at == k) & (lane == i))
            part = jnp.where(here, total, part)
    part_ref[...] = part


def combine_body(entries, count, *refs):
    gram_ref, row_ref, *vectors = refs[: 3 + STEPS]
    basis_out, hess_out, norm_ref, sure_ref = refs[3 + STEPS :]
    shift = shift_of(row_ref[...], count)
    gram = gram_ref[...] / entries
    size = jnp.abs(gram)
    at = lax.broadcasted_iota(jnp.int32, gram.shape, 0)
    lane = lax.broadcasted_iota(jnp.int32, gram.shape, 1)

    def across(values):
        return jnp.sum(values, axis=1, keepdims=True)

    def turned(column):
        return jnp.sum(jnp.where(at == lane, column, 0.0), axis=0, keepdims=True)

    def times(matrix, row):
        return turned(across(matrix * row))

    first = lane[0:1]
    norm = jnp.sqrt(gram[0:1, 0:1] + EPS)
    norm_ref[...] = jnp.broadcast_to(norm, (1, LANES))
    newest = jnp.where(first == 0, 1.0 / norm, 0.0)
    known = jnp.where(at == 0, newest, 0.0)
    sure = jnp.full((1, 1), 1.0, f32)
    for j in range(STEPS):
        moved = pltpu.roll(jnp.broadcast_to(newest, (8, LANES)), 1, 1)[0:1]
        image = moved + shift * newest
        inner = across(known * times(gram, image))
        reduced = image - jnp.sum(known * inner, axis=0, keepdims=True)
        square = across(reduced * times(gram, reduced))
        terms = across(jnp.abs(reduced) * times(size, jnp.abs(reduced)))
        sure = jnp.where(square > KEPT * terms, sure, 0.0)
        below = jnp.sqrt(jnp.maximum(square, 0.0) + EPS)
        column = jnp.where(first <= j, turned(inner), 0.0)
        hess_out[j : j + 1, :] = jnp.where(first == j + 1, below, column)
        newest = reduced / below
        known = jnp.where(at == j + 1, newest, known)
    sure_ref[...] = jnp.broadcast_to(sure, (1, LANES))
    vectors = [v[...] for v in vectors]
    for j in range(STEPS + 1):
        value = known[j : j + 1, 0:1] * vectors[0]
        for k in range(1, j + 1):
            value = value + known[j : j + 1, k : k + 1] * vectors[k]
        basis_out[j] = value


def first_body(*refs):
    *blocks, u_ref, hits_ref, main_ref, rest_ref, c_ref, part_ref, pool_ref = refs
    c = operate(blocks, hits_ref, main_ref, rest_ref, pool_ref)
    c_ref[...] = c
    u = u_ref[...]
    part_ref[...] = row_of({UC: u * c, UU: u * u, CC: c * c})


def advance(entries, row, u, c, known, basis):
    scale, step = lane_of(known, SCALE), lane_of(known, STEP)
    norm = jnp.sqrt(lane_of(row, UU) / entries + EPS / (scale * scale))
    inverse = 1.0 / norm
    here = u * inverse
    image = c * inverse
    lane = lax.broadcasted_iota(jnp.int32, (1, LANES), 1)
    own = lane_of(row, UC) * inverse * inverse / entries
    column = jnp.where(lane < STEPS, row * inverse / entries, 0.0)
    column = jnp.where(lane.astype(f32) == step, own, column)
    scale_next = jnp.sqrt(lane_of(row, CC) * inverse * inverse / entries + EPS)
    reduced = image - own * here
    for i in range(STEPS):
        reduced = reduced - lane_of(row, i) * inverse / entries * basis[i]
    return here, image, inverse, own, column, scale * norm, reduced / scale_next, scale_next


def place(out_ref, in_ref, step, value):
    for i in range(in_ref.shape[0]):
        out_ref[i] = jnp.where(step == i, value, in_ref[i])


def record(hess_out, hess_ref, step, column, below):
    at = lax.broadcasted_iota(jnp.int32, hess_ref.shape, 0).astype(f32)
    lane = lax.broadcasted_iota(jnp.int32, hess_ref.shape, 1).astype(f32)
    hess = jnp.where(at == step, column, hess_ref[...])
    hess_out[...] = jnp.where((at == STEPS) & (lane == step), below, hess)


def numbers(shift, scale, step):
    lane = lax.broadcasted_iota(jnp.int32, (1, LANES), 1)
    row = jnp.where(lane == SHIFT, shift, jnp.zeros((1, LANES), f32))
    row = jnp.where(lane == SCALE, scale, row)
    return jnp.where(lane == STEP, step, row)


def next_body(entries, *refs):
    *blocks, hits_ref, main_ref, rest_ref, sums_ref, u_ref, c_ref, known_ref = refs[:-12]
    basis_ref, images_ref, hess_ref, basis_out, images_out, hess_out = refs[-12:-6]
    u_out, c_out, v_out, known_out, part_ref, pool_ref = refs[-6:]
    w = operate(blocks, hits_ref, main_ref, rest_ref, pool_ref)
    known = known_ref[...]
    step = lane_of(known, STEP)
    row = totals(sums_ref)
    here, image, inverse, own, column, below, u, scale = advance(
        entries, row, u_ref[...], c_ref[...], known, basis_ref
    )
    moved = w * inverse - (own - lane_of(known, SHIFT)) * image
    for i in range(STEPS):
        moved = moved - lane_of(row, i) * inverse / entries * images_ref[i]
    c = moved / scale
    place(basis_out, basis_ref, step, here)
    place(images_out, images_ref, step, image)
    record(hess_out, hess_ref, step, column, below)
    u_out[...] = u
    c_out[...] = c
    v_out[...] = c - own * u
    known_out[...] = numbers(own, scale, step + 1.0)
    products = {i: jnp.where(step == i, here, basis_ref[i]) * c for i in range(STEPS)}
    products.update({UC: u * c, UU: u * u, CC: c * c})
    part_ref[...] = row_of(products)


def last_body(entries, sums_ref, u_ref, c_ref, known_ref, basis_ref, hess_ref, *outs):
    basis_out, hess_out, u_out, known_out, part_ref = outs
    known = known_ref[...]
    step = lane_of(known, STEP)
    here, _, _, own, column, below, u, scale = advance(
        entries, totals(sums_ref), u_ref[...], c_ref[...], known, basis_ref
    )
    place(basis_out, basis_ref, step, here)
    record(hess_out, hess_ref, step, column, below)
    u_out[...] = u
    known_out[...] = numbers(own, scale, step + 1.0)
    part_ref[...] = row_of({UU: u * u})


def finish_body(entries, sums_ref, u_ref, known_ref, basis_ref, hess_ref, basis_out, hess_out, norm_ref):
    scale = lane_of(known_ref[...], SCALE)
    norm = jnp.sqrt(lane_of(totals(sums_ref), UU) / entries + EPS / (scale * scale))
    for i in range(STEPS):
        basis_out[i] = basis_ref[i]
    basis_out[STEPS] = u_ref[...] / norm
    lane = lax.broadcasted_iota(jnp.int32, (1, LANES), 1)
    norms = hess_ref[STEPS : STEPS + 1, :]
    for j in range(STEPS):
        below = lane_of(norms, j + 1) if j + 1 < STEPS else scale * norm
        hess_out[j : j + 1, :] = jnp.where(lane == j + 1, below, hess_ref[j : j + 1, :])
    norm_ref[...] = norms


def shifted(array, d_dom, d_blk):
    doms, blks = lax.axis_size("dom"), lax.axis_size("blk")
    if d_dom == 0 and d_blk == 0:
        return array
    pairs = []
    for d in range(doms):
        for b in range(blks):
            source = ((d + d_dom) % doms) * blks + (b + d_blk) % blks
            pairs.append((source, d * blks + b))
    return lax.ppermute(array, ("dom", "blk"), pairs)


def around(array, reach):
    blks = lax.axis_size("blk")
    whole = jnp.concatenate([shifted(array, 0, b) for b in range(blks)], 0)
    return [shifted(whole, d, 0) for d in range(-reach, reach + 1)]


def added(part, beside=()):
    beside = list(beside)
    doms, blks = lax.axis_size("dom"), lax.axis_size("blk")
    devices = doms * blks
    reach = 1
    while reach < devices:
        ways = 4 if reach * 4 <= devices else 2
        others = [
            lax.ppermute(part, ("dom", "blk"), [(n ^ (k * reach), n) for n in range(devices)])
            for k in range(1, ways)
        ]
        work = beside.pop(0) if beside else None
        zeros = work(part) if work is not None else None
        if ways == 4:
            part = (part + others[0]) + (others[1] + others[2])
        else:
            part = part + others[0]
        if zeros is not None:
            part = part + zeros
        reach *= ways
    for work in beside:
        part = part + work(part)
    return part


def matrices_of(jacobian, line_pivots, line_lower, line_upper):
    elems, faces, cols, _ = jacobian.shape
    lines, levels = line_pivots.shape[:2]
    height = levels * ROWS
    token = jax.ShapeDtypeStruct((1, LANES), f32)
    kept = {}

    def pack(after=None):
        main, rest, done = call(
            pack_body,
            [vmem_out((faces, cols, elems, LANES)), vmem_out((cols, elems, LANES)), token],
            in_hbm(jnp.transpose(jacobian, (1, 2, 0, 3))),
            specs=[pl.BlockSpec(memory_space=pltpu.VMEM if INTERPRET else pltpu.HBM)],
            limit=8,
            after=after,
        )
        kept["jac"] = in_vmem(main), in_vmem(rest)
        return done

    pivots = jnp.transpose(line_pivots, (0, 2, 1, 3)).reshape(lines, cols * levels, cols)
    lower = jnp.transpose(line_lower, (1, 2, 0, 3)).reshape(levels - 1, cols * lines, cols)
    upper = jnp.transpose(line_upper, (1, 2, 0, 3)).reshape(levels - 1, cols * lines, cols)

    def invert(l, after=None):
        main, rest, done = call(
            functools.partial(invert_body, l, lines),
            [vmem_out((levels, height, LANES)), vmem_out((height, LANES)), token],
            pivots,
            lower,
            upper,
            scratch=[
                pltpu.VMEM((levels, height, cols), f32),
                pltpu.VMEM(((levels + lines) * cols, LANES), f32),
                pltpu.VMEM(((levels + lines) * cols, LANES), f32),
            ],
            limit=20,
            after=after,
        )
        kept[l] = in_vmem(main), in_vmem(rest)
        return done

    def lay_out(_):
        anywhere = pl.BlockSpec(memory_space=pl.ANY)
        return call(zero_body, token, lower, upper, specs=[anywhere] * 2)

    return lay_out, invert, pack, kept


def per_device(residual, recycle_basis, recycle_images, jacobian, neighbours, line_members,
               line_pivots, line_lower, line_upper):
    elems, cols = residual.shape
    doms, blks = lax.axis_size("dom"), lax.axis_size("blk")
    lines, levels = line_pivots.shape[:2]
    entries = float(elems * cols * doms * blks)
    count = float(elems * SAMPLE * doms * blks)
    dom, blk = lax.axis_index("dom"), lax.axis_index("blk")
    devices = doms * blks
    row = jax.ShapeDtypeStruct((1, LANES), f32)
    rows = jax.ShapeDtypeStruct((elems, cols), f32)

    members = line_members.reshape(devices, elems)
    near = jnp.array([(d, b) for d in range(-2, 3) for b in range(blks)], jnp.int32)
    at = (dom + near[:, 0] + doms) % doms * blks + (blk + near[:, 1]) % blks
    line_ids = members[at].reshape(-1)
    near_own = at[blks : 4 * blks]
    elem_ids = (near_own[:, None] * elems + jnp.arange(elems, dtype=jnp.int32)).reshape(-1)
    me = dom * blks + blk
    own_ids = me * elems + jnp.arange(elems, dtype=jnp.int32)
    wanted = jnp.concatenate([own_ids[None], neighbours.T], 0).reshape(-1)
    stencil = (wanted[:, None] == line_ids[None, :]).astype(f32)
    mine = lax.dynamic_slice_in_dim(members, me, 1, 0)[0]
    entering = (mine[:, None] == elem_ids[None, :]).astype(f32)
    stencil_pool = pltpu.VMEM((stencil.shape[1], cols), f32)

    jac = jnp.transpose(jacobian, (1, 2, 0, 3))
    pivots = jnp.transpose(line_pivots, (0, 2, 1, 3)).reshape(lines, cols * levels, cols)
    wide = SAMPLE * levels
    part = call(
        project_body,
        row,
        *map(in_hbm, (recycle_images, residual, jac, pivots)),
        specs=[pl.BlockSpec(memory_space=pltpu.VMEM if INTERPRET else pltpu.HBM)] * 4,
        scratch=[]
        if INTERPRET
        else [
            pltpu.VMEM(recycle_images.shape, f32),
            pltpu.VMEM(residual.shape, f32),
            pltpu.VMEM((SAMPLE, elems, cols), f32),
            pltpu.VMEM((lines, wide, cols), f32),
            pltpu.SemaphoreType.DMA((4,)),
        ],
    )
    lay_out, invert, pack, kept = matrices_of(jacobian, line_pivots, line_lower, line_upper)
    inverts = [functools.partial(invert, l) for l in range(lines)]
    projected = added(part, [lay_out, None, *inverts])
    correction, start = call(
        functools.partial(deflate_body, entries),
        [rows, rows],
        projected,
        residual,
        recycle_basis,
        recycle_images,
    )

    pack(start)

    def precondition(v, kept):
        z = call(
            functools.partial(solve_body, lines),
            rows,
            *around(v, 1),
            entering,
            *[kept[l][0] for l in range(lines)],
            *[kept[l][1] for l in range(lines)],
            scratch=[
                pltpu.VMEM((entering.shape[1], cols), f32),
                pltpu.VMEM((elems, ROWS, LANES), f32),
            ],
        )
        return around(z, 2)

    vectors = [start]
    matrix = jax.ShapeDtypeStruct((2 * STEPS, LANES), f32)
    for j in range(STEPS):
        last = j == STEPS - 1
        pool = precondition(vectors[-1], kept)
        result = call(
            functools.partial(power_last_body if last else power_body, count),
            [rows, matrix] if last else rows,
            *pool,
            *(vectors if last else ()),
            vectors[-1],
            projected,
            stencil,
            *kept["jac"],
            scratch=[stencil_pool],
        )
        vectors.append(result[0] if last else result)
    gram = added(result[1])
    small = jax.ShapeDtypeStruct((STEPS, LANES), f32)
    stacked = jax.ShapeDtypeStruct((STEPS + 1, elems, cols), f32)
    basis, hessenberg, norm, sure = call(
        functools.partial(combine_body, entries, count),
        [stacked, small, row, row],
        gram,
        projected,
        *vectors,
    )

    def stepwise(start):
        _, invert, pack, kept = matrices_of(jacobian, line_pivots, line_lower, line_upper)
        for l in range(lines):
            invert(l)
        pack()
        matrices = (stencil, *kept["jac"])
        c, part = call(
            first_body,
            [rows, row],
            *precondition(start, kept),
            start,
            *matrices,
            scratch=[stencil_pool],
        )
        stack = jax.ShapeDtypeStruct((STEPS, elems, cols), f32)

        def step(_, state):
            basis, images, hessenberg, u, c, v, known, part = state
            return tuple(
                call(
                    functools.partial(next_body, entries),
                    [stack, stack, matrix, rows, rows, rows, row, row],
                    *precondition(v, kept),
                    *matrices,
                    added(part),
                    u,
                    c,
                    known,
                    basis,
                    images,
                    hessenberg,
                    scratch=[stencil_pool],
                )
            )

        empty = jnp.zeros(stack.shape, f32)
        known = jnp.zeros((1, LANES), f32).at[0, SCALE].set(1.0)
        state = (empty, empty, jnp.zeros(matrix.shape, f32), start, c, c, known, part)
        basis, _, hessenberg, u, c, _, known, part = lax.fori_loop(0, STEPS - 1, step, state)
        basis, hessenberg, u, known, part = call(
            functools.partial(last_body, entries),
            [stack, matrix, rows, row, row],
            added(part),
            u,
            c,
            known,
            basis,
            hessenberg,
        )
        return tuple(
            call(
                functools.partial(finish_body, entries),
                [stacked, small, row],
                added(part),
                u,
                known,
                basis,
                hessenberg,
            )
        )

    basis, hessenberg, norm = lax.cond(
        sure[0, 0] > 0.5, lambda start: (basis, hessenberg, norm), stepwise, start
    )
    return correction, basis, hessenberg[:, : STEPS + 1].T, norm[0, 0]


def solution(mesh):
    both = ("dom", "blk")
    in_specs = (
        P(both, None),
        P(None, both, None),
        P(None, both, None),
        P(both, None, None, None),
        P(both, None),
        P(),
        P(both, None, None, None),
        P(both, None, None, None),
        P(both, None, None, None),
    )
    out_specs = (P(both, None), P(None, both, None), P(), P())
    return jax.shard_map(
        per_device, mesh=mesh, in_specs=in_specs, out_specs=out_specs, check_vma=False
    )
```

```python
import functools

import jax
import jax.numpy as jnp
from jax import lax
from jax.experimental import pallas as pl
from jax.experimental.pallas import tpu as pltpu
from jax.sharding import PartitionSpec as P

STEPS = 8
EPS = 1e-06
KEPT = 2e-3
SAMPLE = 16
LANES = 128
ROWS = 136
INTERPRET = False
f32 = jnp.float32
bf16 = jnp.bfloat16
MIB = 1024 * 1024


def vmem_out(shape):
    if INTERPRET:
        return jax.ShapeDtypeStruct(shape, f32)
    return pltpu.VMEM(shape, f32)


def in_vmem(array):
    return array if INTERPRET else pltpu.with_memory_space_constraint(array, pltpu.VMEM)


def in_hbm(array):
    return array if INTERPRET else pltpu.with_memory_space_constraint(array, pltpu.HBM)


def call(body, out_shape, *args, scratch=(), limit=8, specs=None, after=None):
    spec = pl.BlockSpec(memory_space=pltpu.VMEM)
    specs = list(specs) if specs is not None else [spec] * len(args)
    inner, count = body, len(args)
    if after is not None:
        specs, args = specs + [pl.BlockSpec(memory_space=pl.ANY)], (*args, after)

        def body(*refs):
            inner(*refs[:count], *refs[count + 1 :])

    outs = out_shape if isinstance(out_shape, (list, tuple)) else None
    return pl.pallas_call(
        body,
        out_shape=out_shape,
        in_specs=specs,
        out_specs=[spec] * len(outs) if outs is not None else spec,
        scratch_shapes=list(scratch),
        compiler_params=pltpu.CompilerParams(vmem_limit_bytes=limit * MIB),
        interpret=INTERPRET,
    )(*args)


def pick(hits, pool):
    hits = hits.astype(bf16)
    high = pool.astype(bf16)
    rest = pool - high.astype(f32)
    mid = rest.astype(bf16)
    low = (rest - mid.astype(f32)).astype(bf16)
    dot = functools.partial(jnp.dot, preferred_element_type=f32)
    return dot(hits, high) + (dot(hits, mid) + dot(hits, low))


def halves(array):
    high = array.astype(bf16)
    return high, (array - high.astype(f32)).astype(bf16)


def product(left, right, dims):
    lh, ll = halves(left)
    rh, rl = halves(right)
    dot = lambda a, b: lax.dot_general(a, b, (dims, ((), ())), preferred_element_type=f32)
    return dot(lh, rh) + (dot(lh, rl) + dot(ll, rh))


def zero_body(*refs):
    refs[-1][...] = jnp.zeros(refs[-1].shape, f32)


def pack_body(jac_hbm, main_ref, rest_ref, token_ref):
    faces, rows, elems, cols = jac_hbm.shape
    chunk, group = 27, 9
    token_ref[...] = jnp.zeros(token_ref.shape, f32)
    extra = cols - LANES

    def step(block, at=None):
        at = (pl.program_id(0) if at is None else at) * chunk
        lane = lax.broadcasted_iota(jnp.int32, (elems, LANES), 1)

        def row(i):
            packed = jnp.zeros((elems, LANES), f32)
            for f in range(faces):
                main_ref[f, at + i] = block[f, i, :, 0:LANES]
                tail = jnp.concatenate(
                    [block[f, i, :, LANES:cols], jnp.zeros((elems, LANES - extra), f32)], 1
                )
                if f:
                    tail = pltpu.roll(tail, f * extra, 1)
                packed = packed + tail
            rest_ref[at + i] = packed

        def some(g, _):
            for n in range(group):
                row(g * group + n)
            return 0

        lax.fori_loop(0, chunk // group, some, 0)

    if INTERPRET:
        for c in range(rows // chunk):
            step(jac_hbm[:, c * chunk : (c + 1) * chunk], c)
        return
    pltpu.emit_pipeline(
        step,
        grid=(rows // chunk,),
        in_specs=[pl.BlockSpec((faces, chunk, elems, cols), lambda c: (0, c, 0, 0))],
    )(jac_hbm)


def invert_body(l, lines, pivot_ref, lower_ref, upper_ref, main_ref, rest_ref, token_ref, part_ref, wide_ref, side_ref):
    levels, height, _ = main_ref.shape
    cols = part_ref.shape[2]
    extra = cols - LANES
    rows_by_rows = ((1,), (1,))
    rows_by_cols = ((1,), (0,))
    pivot_rows = levels * cols
    token_ref[...] = jnp.zeros(token_ref.shape, f32)
    wide_ref[0:pivot_rows, :] = pivot_ref[l, :, 0:LANES]
    side_ref[0:pivot_rows, 0:extra] = pivot_ref[l, :, LANES:cols]

    def strided(first, count):
        at = pl.ds(first, cols, stride=count)
        return jnp.concatenate([wide_ref[at, :], side_ref[at, :][:, 0:extra]], 1)

    def paired(ref, k):
        wide_ref[pivot_rows:, :] = ref[k, :, 0:LANES]
        side_ref[pivot_rows:, 0:extra] = ref[k, :, LANES:cols]
        return strided(pivot_rows + l, lines)

    part_ref[...] = jnp.zeros(part_ref.shape, f32)
    part_ref[0, 0:cols, :] = strided(0, levels).T
    for k in range(1, levels):
        pivot = strided(k, levels)
        mixed = product(pivot, paired(lower_ref, k - 1), rows_by_cols)
        before = part_ref[k - 1, 0 : k * ROWS, :]
        part_ref[k, 0 : k * ROWS, :] = -product(before, mixed, rows_by_rows)
        part_ref[k, k * ROWS : k * ROWS + cols, :] = pivot.T

    def backward(i, _):
        k = levels - 2 - i
        part_ref[k] = part_ref[k] - product(part_ref[k + 1], paired(upper_ref, k), rows_by_rows)
        return 0

    lax.fori_loop(0, levels - 1, backward, 0)

    def emit(t, _):
        at = pl.ds(pl.multiple_of(t * ROWS, 8), ROWS)
        packed = jnp.zeros((ROWS, LANES), f32)
        for k in range(levels):
            main_ref[k, at, :] = part_ref[k, at, 0:LANES]
            tail = jnp.concatenate(
                [part_ref[k, at, LANES:cols], jnp.zeros((ROWS, LANES - extra), f32)], 1
            )
            packed = packed + (pltpu.roll(tail, k * extra, 1) if k else tail)
        rest_ref[at, :] = packed
        return 0

    lax.fori_loop(0, levels, emit, 0)


def solve_body(lines, *refs):
    blocks, refs = refs[: -4 - 2 * lines], refs[-4 - 2 * lines :]
    hits_ref, out_ref, pool_ref, wide_ref = refs[0], *refs[-3:]
    mains, rests = refs[1 : 1 + lines], refs[1 + lines : 1 + 2 * lines]
    levels = mains[0].shape[0]
    count = hits_ref.shape[0]
    cols = pool_ref.shape[1]
    extra = cols - LANES
    fill_pool(blocks, pool_ref)
    rhs = pick(hits_ref[...], pool_ref[...])
    rhs = jnp.concatenate([rhs, jnp.zeros((count, 2 * LANES - cols), f32)], 1)
    rhs = rhs.T[0:ROWS]
    for q in range(count):
        wide_ref[q] = jnp.broadcast_to(rhs[:, q : q + 1], (ROWS, LANES))
    for l in range(lines):

        def member(m, sums):
            sums = list(sums)
            for t in range(ROWS // 8):
                at = pl.ds(pl.multiple_of(m * ROWS + t * 8, 8), 8)
                value = wide_ref[l * levels + m, t * 8 : t * 8 + 8, :]
                for k in range(levels):
                    sums[k] = sums[k] + mains[l][k, at, :] * value
                sums[levels] = sums[levels] + rests[l][at, :] * value
            return tuple(sums)

        zero = jnp.zeros((8, LANES), f32)
        sums = lax.fori_loop(0, levels, member, (zero,) * (levels + 1))
        tails = jnp.sum(sums[levels], axis=0, keepdims=True)
        tails = jnp.broadcast_to(tails, (8, LANES))
        for k in range(levels):
            total = jnp.sum(sums[k], axis=0, keepdims=True)
            tail = pltpu.roll(tails, LANES - k * extra, 1) if k else tails
            at = slice(l * levels + k, l * levels + k + 1)
            out_ref[at, 0:LANES] = total
            out_ref[at, LANES:cols] = tail[0:1, 0:extra]


def fill_pool(blocks, pool_ref):
    at = 0
    for block in blocks:
        count = block.shape[0]
        pool_ref[at : at + count, :] = block[...]
        at += count


def operate(blocks, hits_ref, main_ref, rest_ref, pool_ref):
    faces, rows, elems, _ = main_ref.shape
    cols = pool_ref.shape[1]
    extra = cols - LANES
    fill_pool(blocks, pool_ref)
    field = pick(hits_ref[...], pool_ref[...])
    heads = [field[f * elems : (f + 1) * elems, 0:LANES] for f in range(faces)]
    packed = jnp.zeros((elems, LANES), f32)
    for f in range(faces):
        tail = jnp.concatenate(
            [field[f * elems : (f + 1) * elems, LANES:cols], jnp.zeros((elems, LANES - extra), f32)], 1
        )
        packed = packed + (pltpu.roll(tail, f * extra, 1) if f else tail)
    lane = lax.broadcasted_iota(jnp.int32, (elems, LANES), 1)

    def one(i):
        total = rest_ref[i] * packed
        for f in range(faces):
            total = total + main_ref[f, i] * heads[f]
        return jnp.sum(total, axis=1, keepdims=True)

    group = 16

    def some(g, image):
        for s in range(group):
            i = g * group + s
            image = jnp.where(lane == i, one(i), image)
        return image

    image = lax.fori_loop(0, LANES // group, some, jnp.zeros((elems, LANES), f32))
    tail = jnp.zeros((elems, LANES), f32)
    for c in range(extra):
        tail = jnp.where(lane == c, one(LANES + c), tail)
    return jnp.concatenate([image, tail[:, 0:extra]], 1)


def row_of(values):
    lane = lax.broadcasted_iota(jnp.int32, (1, LANES), 1)
    row = jnp.zeros((1, LANES), f32)
    for i, value in values.items():
        total = jnp.sum(jnp.sum(value, axis=0, keepdims=True), axis=1, keepdims=True)
        row = jnp.where(lane == i, total, row)
    return row


def lane_of(row, i):
    return row[:, i : i + 1]


UC, UU, CC = 13, 14, 15
SHIFT, SCALE, STEP = 0, 1, 2


def totals(parts_ref):
    return jnp.sum(parts_ref[...], axis=0, keepdims=True)


def project_body(images_in, residual_in, jac_in, pivot_in, out_ref, *refs):
    lines, levels = pivot_in.shape[0], pivot_in.shape[1] // jac_in.shape[1]
    sources = [
        images_in,
        residual_in,
        jac_in.at[0, 0:SAMPLE],
        pivot_in.at[:, 0 : SAMPLE * levels, :],
    ]
    if INTERPRET:
        refs = [source[...] for source in sources]
    else:
        *refs, sems = refs
        copies = [
            pltpu.make_async_copy(source, ref, sems.at[n])
            for n, (source, ref) in enumerate(zip(sources, refs))
        ]
        for copy in copies:
            copy.start()
        for copy in copies:
            copy.wait()
    images_ref, residual_ref, jac_ref, pivot_ref = refs
    residual = residual_ref[...]
    products = {k: images_ref[k] * residual for k in range(STEPS)}
    lane = lax.broadcasted_iota(jnp.int32, jac_ref.shape[1:], 1)
    own = jnp.zeros(jac_ref.shape[1:], f32)
    for i in range(SAMPLE):
        own = jnp.where(lane == i, jac_ref[i], own)
    products[STEPS] = own
    shape = (levels, pivot_ref.shape[2])
    lane = lax.broadcasted_iota(jnp.int32, shape, 1)
    own = jnp.zeros(shape, f32)
    for l in range(lines):
        for i in range(SAMPLE):
            own = own + jnp.where(lane == i, pivot_ref[l, i * levels : (i + 1) * levels], 0.0)
    products[STEPS + 1] = own
    out_ref[...] = row_of(products)


def deflate_body(entries, parts_ref, residual_ref, basis_ref, images_ref, correction_ref, start_ref):
    row = totals(parts_ref) / entries
    correction = jnp.zeros(residual_ref.shape, f32)
    start = residual_ref[...]
    for k in range(basis_ref.shape[0]):
        weight = lane_of(row, k)
        correction = correction + weight * basis_ref[k]
        start = start - weight * images_ref[k]
    correction_ref[...] = correction
    start_ref[...] = start


def shift_of(row, count):
    return lane_of(row, STEPS) / count * (lane_of(row, STEPS + 1) / count)


def power_body(count, *refs):
    *blocks, u_ref, row_ref, hits_ref, main_ref, rest_ref, out_ref, pool_ref = refs
    image = operate(blocks, hits_ref, main_ref, rest_ref, pool_ref)
    out_ref[...] = image - shift_of(row_ref[...], count) * u_ref[...]


def power_last_body(count, *refs):
    blocks, vectors, refs = refs[: -8 - STEPS], refs[-8 - STEPS : -8], refs[-8:]
    u_ref, row_ref, hits_ref, main_ref, rest_ref, out_ref, part_ref, pool_ref = refs
    image = operate(blocks, hits_ref, main_ref, rest_ref, pool_ref)
    last = image - shift_of(row_ref[...], count) * u_ref[...]
    out_ref[...] = last
    vectors = [v[...] for v in vectors] + [last]
    at = lax.broadcasted_iota(jnp.int32, part_ref.shape, 0)
    lane = lax.broadcasted_iota(jnp.int32, part_ref.shape, 1)
    part = jnp.zeros(part_ref.shape, f32)
    for k, right in enumerate(vectors):
        for i in range(k + 1):
            total = jnp.sum(vectors[i] * right, axis=0, keepdims=True)
            total = jnp.sum(total, axis=1, keepdims=True)
            here = ((at == i) & (lane == k)) | ((at == k) & (lane == i))
            part = jnp.where(here, total, part)
    part_ref[...] = part


def combine_body(entries, count, *refs):
    gram_ref, row_ref, *vectors = refs[: 3 + STEPS]
    basis_out, hess_out, norm_ref, sure_ref = refs[3 + STEPS :]
    shift = shift_of(row_ref[...], count)
    gram = gram_ref[...] / entries
    size = jnp.abs(gram)
    at = lax.broadcasted_iota(jnp.int32, gram.shape, 0)
    lane = lax.broadcasted_iota(jnp.int32, gram.shape, 1)

    def across(values):
        return jnp.sum(values, axis=1, keepdims=True)

    def turned(column):
        return jnp.sum(jnp.where(at == lane, column, 0.0), axis=0, keepdims=True)

    def times(matrix, row):
        return turned(across(matrix * row))

    first = lane[0:1]
    norm = jnp.sqrt(gram[0:1, 0:1] + EPS)
    norm_ref[...] = jnp.broadcast_to(norm, (1, LANES))
    newest = jnp.where(first == 0, 1.0 / norm, 0.0)
    known = jnp.where(at == 0, newest, 0.0)
    sure = jnp.full((1, 1), 1.0, f32)
    for j in range(STEPS):
        moved = pltpu.roll(jnp.broadcast_to(newest, (8, LANES)), 1, 1)[0:1]
        image = moved + shift * newest
        inner = across(known * times(gram, image))
        reduced = image - jnp.sum(known * inner, axis=0, keepdims=True)
        square = across(reduced * times(gram, reduced))
        terms = across(jnp.abs(reduced) * times(size, jnp.abs(reduced)))
        sure = jnp.where(square > KEPT * terms, sure, 0.0)
        below = jnp.sqrt(jnp.maximum(square, 0.0) + EPS)
        column = jnp.where(first <= j, turned(inner), 0.0)
        hess_out[j : j + 1, :] = jnp.where(first == j + 1, below, column)
        newest = reduced / below
        known = jnp.where(at == j + 1, newest, known)
    sure_ref[...] = jnp.broadcast_to(sure, (1, LANES))
    vectors = [v[...] for v in vectors]
    for j in range(STEPS + 1):
        value = known[j : j + 1, 0:1] * vectors[0]
        for k in range(1, j + 1):
            value = value + known[j : j + 1, k : k + 1] * vectors[k]
        basis_out[j] = value


def first_body(*refs):
    *blocks, u_ref, hits_ref, main_ref, rest_ref, c_ref, part_ref, pool_ref = refs
    c = operate(blocks, hits_ref, main_ref, rest_ref, pool_ref)
    c_ref[...] = c
    u = u_ref[...]
    part_ref[...] = row_of({UC: u * c, UU: u * u, CC: c * c})


def advance(entries, row, u, c, known, basis):
    scale, step = lane_of(known, SCALE), lane_of(known, STEP)
    norm = jnp.sqrt(lane_of(row, UU) / entries + EPS / (scale * scale))
    inverse = 1.0 / norm
    here = u * inverse
    image = c * inverse
    lane = lax.broadcasted_iota(jnp.int32, (1, LANES), 1)
    own = lane_of(row, UC) * inverse * inverse / entries
    column = jnp.where(lane < STEPS, row * inverse / entries, 0.0)
    column = jnp.where(lane.astype(f32) == step, own, column)
    scale_next = jnp.sqrt(lane_of(row, CC) * inverse * inverse / entries + EPS)
    reduced = image - own * here
    for i in range(STEPS):
        reduced = reduced - lane_of(row, i) * inverse / entries * basis[i]
    return here, image, inverse, own, column, scale * norm, reduced / scale_next, scale_next


def place(out_ref, in_ref, step, value):
    for i in range(in_ref.shape[0]):
        out_ref[i] = jnp.where(step == i, value, in_ref[i])


def record(hess_out, hess_ref, step, column, below):
    at = lax.broadcasted_iota(jnp.int32, hess_ref.shape, 0).astype(f32)
    lane = lax.broadcasted_iota(jnp.int32, hess_ref.shape, 1).astype(f32)
    hess = jnp.where(at == step, column, hess_ref[...])
    hess_out[...] = jnp.where((at == STEPS) & (lane == step), below, hess)


def numbers(shift, scale, step):
    lane = lax.broadcasted_iota(jnp.int32, (1, LANES), 1)
    row = jnp.where(lane == SHIFT, shift, jnp.zeros((1, LANES), f32))
    row = jnp.where(lane == SCALE, scale, row)
    return jnp.where(lane == STEP, step, row)


def next_body(entries, *refs):
    *blocks, hits_ref, main_ref, rest_ref, sums_ref, u_ref, c_ref, known_ref = refs[:-12]
    basis_ref, images_ref, hess_ref, basis_out, images_out, hess_out = refs[-12:-6]
    u_out, c_out, v_out, known_out, part_ref, pool_ref = refs[-6:]
    w = operate(blocks, hits_ref, main_ref, rest_ref, pool_ref)
    known = known_ref[...]
    step = lane_of(known, STEP)
    row = totals(sums_ref)
    here, image, inverse, own, column, below, u, scale = advance(
        entries, row, u_ref[...], c_ref[...], known, basis_ref
    )
    moved = w * inverse - (own - lane_of(known, SHIFT)) * image
    for i in range(STEPS):
        moved = moved - lane_of(row, i) * inverse / entries * images_ref[i]
    c = moved / scale
    place(basis_out, basis_ref, step, here)
    place(images_out, images_ref, step, image)
    record(hess_out, hess_ref, step, column, below)
    u_out[...] = u
    c_out[...] = c
    v_out[...] = c - own * u
    known_out[...] = numbers(own, scale, step + 1.0)
    products = {i: jnp.where(step == i, here, basis_ref[i]) * c for i in range(STEPS)}
    products.update({UC: u * c, UU: u * u, CC: c * c})
    part_ref[...] = row_of(products)


def last_body(entries, sums_ref, u_ref, c_ref, known_ref, basis_ref, hess_ref, *outs):
    basis_out, hess_out, u_out, known_out, part_ref = outs
    known = known_ref[...]
    step = lane_of(known, STEP)
    here, _, _, own, column, below, u, scale = advance(
        entries, totals(sums_ref), u_ref[...], c_ref[...], known, basis_ref
    )
    place(basis_out, basis_ref, step, here)
    record(hess_out, hess_ref, step, column, below)
    u_out[...] = u
    known_out[...] = numbers(own, scale, step + 1.0)
    part_ref[...] = row_of({UU: u * u})


def finish_body(entries, sums_ref, u_ref, known_ref, basis_ref, hess_ref, basis_out, hess_out, norm_ref):
    scale = lane_of(known_ref[...], SCALE)
    norm = jnp.sqrt(lane_of(totals(sums_ref), UU) / entries + EPS / (scale * scale))
    for i in range(STEPS):
        basis_out[i] = basis_ref[i]
    basis_out[STEPS] = u_ref[...] / norm
    lane = lax.broadcasted_iota(jnp.int32, (1, LANES), 1)
    norms = hess_ref[STEPS : STEPS + 1, :]
    for j in range(STEPS):
        below = lane_of(norms, j + 1) if j + 1 < STEPS else scale * norm
        hess_out[j : j + 1, :] = jnp.where(lane == j + 1, below, hess_ref[j : j + 1, :])
    norm_ref[...] = norms


def shifted(array, step):
    doms = lax.axis_size("dom")
    if step == 0:
        return array
    return lax.ppermute(array, "dom", [((d + step) % doms, d) for d in range(doms)])


def masks(blks):
    return [2 * m - 1 for m in (1, 2, 4, 8) if m < blks]


def row_order(blks):
    order = [0]
    for mask in masks(blks):
        order = order + [o ^ mask for o in order]
    return order


def around(array, reach):
    blks = lax.axis_size("blk")
    whole = array
    for mask in masks(blks):
        other = lax.ppermute(whole, "blk", [(b ^ mask, b) for b in range(blks)])
        whole = jnp.concatenate([whole, other], 0)
    return [shifted(whole, d) for d in range(-reach, reach + 1)]


def added(part, beside=()):
    beside = list(beside)
    doms, blks = lax.axis_size("dom"), lax.axis_size("blk")
    devices = doms * blks
    reach = 1
    while reach < devices:
        ways = 4 if reach * 4 <= devices else 2
        others = [
            lax.ppermute(part, ("dom", "blk"), [(n ^ (k * reach), n) for n in range(devices)])
            for k in range(1, ways)
        ]
        work = beside.pop(0) if beside else None
        zeros = work(part) if work is not None else None
        if ways == 4:
            part = (part + others[0]) + (others[1] + others[2])
        else:
            part = part + others[0]
        if zeros is not None:
            part = part + zeros
        reach *= ways
    for work in beside:
        part = part + work(part)
    return part


def matrices_of(jacobian, line_pivots, line_lower, line_upper):
    elems, faces, cols, _ = jacobian.shape
    lines, levels = line_pivots.shape[:2]
    height = levels * ROWS
    token = jax.ShapeDtypeStruct((1, LANES), f32)
    kept = {}

    def pack(after=None):
        main, rest, done = call(
            pack_body,
            [vmem_out((faces, cols, elems, LANES)), vmem_out((cols, elems, LANES)), token],
            in_hbm(jnp.transpose(jacobian, (1, 2, 0, 3))),
            specs=[pl.BlockSpec(memory_space=pltpu.VMEM if INTERPRET else pltpu.HBM)],
            limit=8,
            after=after,
        )
        kept["jac"] = in_vmem(main), in_vmem(rest)
        return done

    pivots = jnp.transpose(line_pivots, (0, 2, 1, 3)).reshape(lines, cols * levels, cols)
    lower = jnp.transpose(line_lower, (1, 2, 0, 3)).reshape(levels - 1, cols * lines, cols)
    upper = jnp.transpose(line_upper, (1, 2, 0, 3)).reshape(levels - 1, cols * lines, cols)

    def invert(l, after=None):
        main, rest, done = call(
            functools.partial(invert_body, l, lines),
            [vmem_out((levels, height, LANES)), vmem_out((height, LANES)), token],
            pivots,
            lower,
            upper,
            scratch=[
                pltpu.VMEM((levels, height, cols), f32),
                pltpu.VMEM(((levels + lines) * cols, LANES), f32),
                pltpu.VMEM(((levels + lines) * cols, LANES), f32),
            ],
            limit=20,
            after=after,
        )
        kept[l] = in_vmem(main), in_vmem(rest)
        return done

    def lay_out(_):
        anywhere = pl.BlockSpec(memory_space=pl.ANY)
        return call(zero_body, token, lower, upper, specs=[anywhere] * 2)

    return lay_out, invert, pack, kept


def per_device(residual, recycle_basis, recycle_images, jacobian, neighbours, line_members,
               line_pivots, line_lower, line_upper):
    elems, cols = residual.shape
    doms, blks = lax.axis_size("dom"), lax.axis_size("blk")
    lines, levels = line_pivots.shape[:2]
    entries = float(elems * cols * doms * blks)
    count = float(elems * SAMPLE * doms * blks)
    dom, blk = lax.axis_index("dom"), lax.axis_index("blk")
    devices = doms * blks
    row = jax.ShapeDtypeStruct((1, LANES), f32)
    rows = jax.ShapeDtypeStruct((elems, cols), f32)

    members = line_members.reshape(devices, elems)
    near = jnp.array([(d, o) for d in range(-2, 3) for o in row_order(blks)], jnp.int32)
    at = (dom + near[:, 0] + doms) % doms * blks + (blk ^ near[:, 1])
    line_ids = members[at].reshape(-1)
    near_own = at[blks : 4 * blks]
    elem_ids = (near_own[:, None] * elems + jnp.arange(elems, dtype=jnp.int32)).reshape(-1)
    me = dom * blks + blk
    own_ids = me * elems + jnp.arange(elems, dtype=jnp.int32)
    wanted = jnp.concatenate([own_ids[None], neighbours.T], 0).reshape(-1)
    stencil = (wanted[:, None] == line_ids[None, :]).astype(f32)
    mine = lax.dynamic_slice_in_dim(members, me, 1, 0)[0]
    entering = (mine[:, None] == elem_ids[None, :]).astype(f32)
    stencil_pool = pltpu.VMEM((stencil.shape[1], cols), f32)

    jac = jnp.transpose(jacobian, (1, 2, 0, 3))
    pivots = jnp.transpose(line_pivots, (0, 2, 1, 3)).reshape(lines, cols * levels, cols)
    wide = SAMPLE * levels
    part = call(
        project_body,
        row,
        *map(in_hbm, (recycle_images, residual, jac, pivots)),
        specs=[pl.BlockSpec(memory_space=pltpu.VMEM if INTERPRET else pltpu.HBM)] * 4,
        scratch=[]
        if INTERPRET
        else [
            pltpu.VMEM(recycle_images.shape, f32),
            pltpu.VMEM(residual.shape, f32),
            pltpu.VMEM((SAMPLE, elems, cols), f32),
            pltpu.VMEM((lines, wide, cols), f32),
            pltpu.SemaphoreType.DMA((4,)),
        ],
    )
    lay_out, invert, pack, kept = matrices_of(jacobian, line_pivots, line_lower, line_upper)
    inverts = [functools.partial(invert, l) for l in range(lines)]
    projected = added(part, [lay_out, None, *inverts])
    correction, start = call(
        functools.partial(deflate_body, entries),
        [rows, rows],
        projected,
        residual,
        recycle_basis,
        recycle_images,
    )

    pack(start)

    def precondition(v, kept):
        z = call(
            functools.partial(solve_body, lines),
            rows,
            *around(v, 1),
            entering,
            *[kept[l][0] for l in range(lines)],
            *[kept[l][1] for l in range(lines)],
            scratch=[
                pltpu.VMEM((entering.shape[1], cols), f32),
                pltpu.VMEM((elems, ROWS, LANES), f32),
            ],
        )
        return around(z, 2)

    vectors = [start]
    matrix = jax.ShapeDtypeStruct((2 * STEPS, LANES), f32)
    for j in range(STEPS):
        last = j == STEPS - 1
        pool = precondition(vectors[-1], kept)
        result = call(
            functools.partial(power_last_body if last else power_body, count),
            [rows, matrix] if last else rows,
            *pool,
            *(vectors if last else ()),
            vectors[-1],
            projected,
            stencil,
            *kept["jac"],
            scratch=[stencil_pool],
        )
        vectors.append(result[0] if last else result)
    gram = added(result[1])
    small = jax.ShapeDtypeStruct((STEPS, LANES), f32)
    stacked = jax.ShapeDtypeStruct((STEPS + 1, elems, cols), f32)
    basis, hessenberg, norm, sure = call(
        functools.partial(combine_body, entries, count),
        [stacked, small, row, row],
        gram,
        projected,
        *vectors,
    )

    def stepwise(start):
        _, invert, pack, kept = matrices_of(jacobian, line_pivots, line_lower, line_upper)
        for l in range(lines):
            invert(l)
        pack()
        matrices = (stencil, *kept["jac"])
        c, part = call(
            first_body,
            [rows, row],
            *precondition(start, kept),
            start,
            *matrices,
            scratch=[stencil_pool],
        )
        stack = jax.ShapeDtypeStruct((STEPS, elems, cols), f32)

        def step(_, state):
            basis, images, hessenberg, u, c, v, known, part = state
            return tuple(
                call(
                    functools.partial(next_body, entries),
                    [stack, stack, matrix, rows, rows, rows, row, row],
                    *precondition(v, kept),
                    *matrices,
                    added(part),
                    u,
                    c,
                    known,
                    basis,
                    images,
                    hessenberg,
                    scratch=[stencil_pool],
                )
            )

        empty = jnp.zeros(stack.shape, f32)
        known = jnp.zeros((1, LANES), f32).at[0, SCALE].set(1.0)
        state = (empty, empty, jnp.zeros(matrix.shape, f32), start, c, c, known, part)
        basis, _, hessenberg, u, c, _, known, part = lax.fori_loop(0, STEPS - 1, step, state)
        basis, hessenberg, u, known, part = call(
            functools.partial(last_body, entries),
            [stack, matrix, rows, row, row],
            added(part),
            u,
            c,
            known,
            basis,
            hessenberg,
        )
        return tuple(
            call(
                functools.partial(finish_body, entries),
                [stacked, small, row],
                added(part),
                u,
                known,
                basis,
                hessenberg,
            )
        )

    basis, hessenberg, norm = lax.cond(
        sure[0, 0] > 0.5, lambda start: (basis, hessenberg, norm), stepwise, start
    )
    return correction, basis, hessenberg[:, : STEPS + 1].T, norm[0, 0]


def solution(mesh):
    both = ("dom", "blk")
    in_specs = (
        P(both, None),
        P(None, both, None),
        P(None, both, None),
        P(both, None, None, None),
        P(both, None),
        P(),
        P(both, None, None, None),
        P(both, None, None, None),
        P(both, None, None, None),
    )
    out_specs = (P(both, None), P(None, both, None), P(), P())
    return jax.shard_map(
        per_device, mesh=mesh, in_specs=in_specs, out_specs=out_specs, check_vma=False
    )
```
